256 devices in a mesh: gx: 32 (over y_lo, z, core), gy: 8 (over x, y_hi).
Axes of the slice: x: 4, y: 4 (y_hi: 2, y_lo: 2; y = y_hi * 2 + y_lo), z: 8, core: 2. Of those that a mesh axis runs over, the one named last changes fastest.
Arguments:
- features: bfloat16 [32, 8, 128, 128], P('gx', 'gy'), may hold values from -6 to 6
- positions: float32 [32, 8, 3, 128], P('gx', 'gy'), may hold values from 0 to 4
- neighbours: int32 [32, 8, 32, 128], P('gx', 'gy'), may hold values from 0 to 287, as said below
- neighbour_counts: int32 [32, 8, 128], P('gx', 'gy'), may hold values from 16 to 32, as said below
- domain_counts: int32 [32, 8], P('gx', 'gy'), may hold values from 64 to 128, as said below
- face_lists: int32 [32, 8, 2, 64], P('gx', 'gy'), may hold values from 0 to 127, as said below
- corner_lists: int32 [32, 8, 2, 16], P('gx', 'gy'), may hold values from 0 to 127, as said below
- w_center: bfloat16 [128, 128], replicated, may hold values from -0.5 to 0.5
- w_neigh: bfloat16 [128, 128], replicated, may hold values from -0.5 to 0.5
- w_radial: float32 [8, 128], replicated, may hold values from -2 to 2
- w_latent: bfloat16 [128, 128], replicated, may hold values from -0.5 to 0.5
- w_readout: bfloat16 [384, 128], replicated, may hold values from -0.3125 to 0.3125
- w_energy: float32 [128], replicated, may hold values from -0.5 to 0.5
Outputs:
- energy: float32 [], replicated
- forces: float32 [32, 8, 3, 128], P('gx', 'gy')
The draws below stay inside these ranges and needn't reach their ends.
Inputs may be any that keep to these rules, and one draw needn't show every extreme that they name: `domain_counts`: each domain's count is at least half its slots, and some domain is full. `neighbour_counts`: some atom of every domain uses all slots. `neighbours`: an index is a live own atom (below the domain's count) or a ghost slot (128 to 287), never the atom itself. `face_lists`: every index is a live atom of the sending domain; an atom may appear more than once. `corner_lists`: every index is a live atom of the sending domain; an atom may appear more than once.
All inputs are finite; a program needn't handle non-finite values.
Results may differ from the reference program's by a relative error of at most 0.011.
Values sent between devices are 32-bit elements; how exact they have to be, the bound alone decides.
A program may use at most 128 MiB of HBM per device.

```python
import math
import jax
import jax.numpy as jnp
from jax import lax

C = 128
NB = 8
NBR = 32
A_DEV = 128
GF = 64
GC = 16
NG = 160
N_GX = 32
N_GY = 8


def domain_table(key):
    count_all = N_GX * N_GY
    base = jax.random.randint(key, (count_all,), A_DEV // 2, A_DEV + 1)
    chosen = jax.random.randint(jax.random.fold_in(key, 101), (), 0, count_all)
    base = jnp.where(jnp.arange(count_all) == chosen, A_DEV, base)
    return base.reshape(N_GX, N_GY).astype(jnp.int32)


def draw_domain_counts(key, part):
    return domain_table(key)


def draw_neighbours(key, part):
    counts = domain_table(key)
    key = jax.random.fold_in(key, 1)
    limit = (counts + NG - 1)[:, :, None, None]
    raw = jax.random.randint(key, (N_GX, N_GY, NBR, A_DEV), 0, limit)
    atom = jnp.arange(A_DEV)[None, None, None, :]
    linear = raw + (raw >= atom).astype(jnp.int32)
    owned = counts[:, :, None, None]
    return jnp.where(linear < owned, linear, A_DEV + linear - owned).astype(jnp.int32)


def draw_neighbour_counts(key, part):
    key = jax.random.fold_in(key, 2)
    base = jax.random.randint(key, (N_GX, N_GY, A_DEV), NBR // 2, NBR + 1)
    chosen = jax.random.randint(jax.random.fold_in(key, 7), (N_GX, N_GY, 1), 0, A_DEV // 2)
    full = jnp.arange(A_DEV)[None, None, :] == chosen
    return jnp.where(full, NBR, base).astype(jnp.int32)


def send_table(key, counts, rows):
    raw = jax.random.randint(key, (N_GX, N_GY, 2, rows), 0, counts[:, :, None, None])
    column = jnp.arange(rows)[None, None, None, :]
    last_live = jnp.broadcast_to((counts - 1)[:, :, None, None], raw.shape)
    raw = jnp.where(column == 0, last_live, raw)
    raw = jnp.where(column == 1, 0, raw)
    return raw.astype(jnp.int32)


def draw_face_lists(key, part):
    counts = domain_table(key)
    key = jax.random.fold_in(key, 3)
    return send_table(key, counts, GF)


def draw_corner_lists(key, part):
    counts = domain_table(key)
    key = jax.random.fold_in(key, 4)
    return send_table(key, counts, GC)


def levels(stream_key, shape, split, least, top_value):
    level = 1.0
    for position, shards_of in split:
        steps = jax.random.uniform(jax.random.fold_in(jax.random.fold_in(stream_key, 6), position), (shards_of,), jnp.float32, least / len(split), top_value / len(split))
        level = level * jnp.repeat(jnp.exp(steps), shape[position] // shards_of).reshape((-1,) + (1,) * (len(shape) - 1 - position))
    return level


def bell_draw(key, dims, spread, most, split=(), held_as=jnp.bfloat16):
    entries = spread * jax.random.normal(key, dims, jnp.float32)
    if split:
        entries = entries * levels(key, dims, split, -0.22, 0.18)
    return jnp.clip(entries, -most, most).astype(held_as)


def setup_inputs(seed: int = 0) -> dict:
    keys = jax.random.split(jax.random.key(seed), 14)
    return {
        "features": bell_draw(keys[0], (N_GX, N_GY, A_DEV, C), 1.0, 6.0, ((0, 32), (1, 8))),
        "positions": jnp.clip(4.0 * jax.random.uniform(keys[1], (N_GX, N_GY, 3, A_DEV), jnp.float32) ** levels(keys[1], (N_GX, N_GY, 3, A_DEV), ((0, 32), (1, 8)), -0.2, 0.2), 0.0, 4.0),
        "neighbours": draw_neighbours(jax.random.fold_in(keys[13], 71), 0),
        "neighbour_counts": draw_neighbour_counts(jax.random.fold_in(keys[13], 71), 0),
        "domain_counts": draw_domain_counts(jax.random.fold_in(keys[13], 71), 0),
        "face_lists": draw_face_lists(jax.random.fold_in(keys[13], 71), 0),
        "corner_lists": draw_corner_lists(jax.random.fold_in(keys[13], 71), 0),
        "w_center": bell_draw(keys[7], (C, C), C ** -0.5, 0.5),
        "w_neigh": bell_draw(keys[8], (C, C), C ** -0.5, 0.5),
        "w_radial": bell_draw(keys[9], (NB, C), NB ** -0.5, 2.0, (), jnp.float32),
        "w_latent": bell_draw(keys[10], (C, C), C ** -0.5, 0.5),
        "w_readout": bell_draw(keys[11], (3 * C, C), (3 * C) ** -0.5, 0.3125),
        "w_energy": bell_draw(keys[12], (C,), C ** -0.5, 0.5, (), jnp.float32),
    }


cutoff = 6.0
soften = 0.25
box_width = 4.0
parity = (1.0, -1.0, -1.0, -1.0, 1.0, 1.0, 1.0, 1.0, 1.0)

def harmonics(unit):
    along_x, along_y, along_z = (unit[0], unit[1], unit[2])
    root3 = math.sqrt(3.0)
    root15 = math.sqrt(15.0)
    root5 = math.sqrt(5.0)
    return jnp.stack([jnp.ones_like(along_x), root3 * along_x, root3 * along_y, root3 * along_z, root15 * along_x * along_y, root15 * along_y * along_z, 0.5 * root5 * (3.0 * along_z * along_z - 1.0), root15 * along_x * along_z, 0.5 * root15 * (along_x * along_x - along_y * along_y)])

def pair_terms(placed, neigh_all, center_proj, nbr_index, pair_live, w_radial, w_latent):
    n_atoms = center_proj.shape[0]
    total_rows = neigh_all.shape[0]
    slots = nbr_index.shape[0]
    width = center_proj.shape[1]
    anchor = placed[:, :n_atoms]
    other = jnp.take(placed, nbr_index, axis=1)
    delta = other - anchor[:, None, :]
    radius = jnp.sqrt(lax.optimization_barrier(jnp.sum(delta * delta, axis=0)) + soften)
    unit = delta / radius[None]
    scaled = jnp.minimum(radius / cutoff, 1.0)
    envelope = 1.0 - 28.0 * scaled ** 6 + 48.0 * scaled ** 7 - 21.0 * scaled ** 8
    orders = jnp.arange(1, w_radial.shape[0] + 1).astype(jnp.float32)
    basis = math.sqrt(2.0 / cutoff) * jnp.sin(orders[:, None, None] * (math.pi / cutoff) * radius[None]) / radius[None]
    radial = jnp.einsum('nka,nc->kac', basis, w_radial, precision=lax.Precision.HIGHEST)
    pre_act = center_proj[None] + jnp.take(neigh_all, nbr_index, axis=0) + radial
    hidden = jax.nn.silu(pre_act).astype(jnp.bfloat16)
    latent = jax.nn.silu(jnp.dot(hidden.reshape(slots * n_atoms, width), w_latent, preferred_element_type=jnp.float32)).reshape(slots, n_atoms, width)
    weight = latent * (envelope * pair_live)[:, :, None]
    harm = harmonics(unit)
    center_sum = jnp.einsum('mka,kac->amc', harm, weight, precision=lax.Precision.HIGHEST).reshape(n_atoms, 9 * width)
    block = math.gcd(slots, 8)
    groups = slots // block
    signs = jnp.array(parity, dtype=jnp.float32)
    signed = jnp.transpose((harm * signs[:, None, None]).reshape(9, groups, block * n_atoms), (1, 0, 2))
    weight_blocks = weight.reshape(groups, block * n_atoms, width)
    index_blocks = nbr_index.reshape(groups, block * n_atoms)

    def add_block(carry, item):
        harm_block, weight_block, index_block = item
        term = (jnp.transpose(harm_block)[:, :, None] * weight_block[:, None, :]).reshape(-1, 9 * width)
        return (carry + jax.ops.segment_sum(term, index_block, num_segments=total_rows), None)
    start = jnp.zeros((total_rows, 9 * width), dtype=weight.dtype)
    scattered, unused = lax.scan(add_block, start, (signed, weight_blocks, index_blocks))
    return scattered.at[:n_atoms, :].add(center_sum)

def readout(moments, atom_live, w_readout, w_energy):
    n_atoms = moments.shape[0]
    shaped = moments.reshape(n_atoms, 9, -1)
    squares = shaped * shaped
    invariants = jnp.stack([jnp.log1p(squares[:, 0]), jnp.log1p(lax.optimization_barrier(jnp.sum(squares[:, 1:4], axis=1))), jnp.log1p(lax.optimization_barrier(jnp.sum(squares[:, 4:9], axis=1)))], axis=1)
    packed = invariants.reshape(n_atoms, -1).astype(jnp.bfloat16)
    hidden = jax.nn.silu(jnp.dot(packed, w_readout, preferred_element_type=jnp.float32))
    energies = jnp.dot(hidden, w_energy, precision=lax.Precision.HIGHEST)
    return jnp.sum(energies * atom_live)

def twice(func):
    return jax.vmap(jax.vmap(func))

def cut_groups(array, axis):
    first = lax.slice_in_dim(array, 0, GF, axis=axis)
    second = lax.slice_in_dim(array, GF, 2 * GF, axis=axis)
    third = lax.slice_in_dim(array, 2 * GF, 2 * GF + GC, axis=axis)
    fourth = lax.slice_in_dim(array, 2 * GF + GC, NG, axis=axis)
    return (first, second, third, fourth)

def to_holders(array, axis):
    first, second, third, fourth = cut_groups(array, axis)
    return jnp.concatenate([jnp.roll(first, -1, 0), jnp.roll(second, -1, 1), jnp.roll(third, (-1, -1), (0, 1)), jnp.roll(fourth, (-1, 1), (0, 1))], axis=axis)

def to_owners(array, axis):
    first, second, third, fourth = cut_groups(array, axis)
    return jnp.concatenate([jnp.roll(first, 1, 0), jnp.roll(second, 1, 1), jnp.roll(third, (1, 1), (0, 1)), jnp.roll(fourth, (1, -1), (0, 1))], axis=axis)

def ghost_offsets():
    shift_x = jnp.concatenate([jnp.full((GF,), box_width), jnp.zeros((GF,)), jnp.full((2 * GC,), box_width)])
    shift_y = jnp.concatenate([jnp.zeros((GF,)), jnp.full((GF,), box_width), jnp.full((GC,), box_width), jnp.full((GC,), -box_width)])
    return jnp.stack([shift_x, shift_y, jnp.zeros((NG,))]).astype(jnp.float32)

def reference(features, positions, neighbours, neighbour_counts, domain_counts, face_lists, corner_lists, w_center, w_neigh, w_radial, w_latent, w_readout, w_energy):
    domains = N_GX * N_GY
    rows_all = A_DEV + NG
    center_proj = jnp.dot(features.reshape(-1, C), w_center, preferred_element_type=jnp.float32).reshape(N_GX, N_GY, A_DEV, C)
    neigh_proj = jnp.dot(features.reshape(-1, C), w_neigh, preferred_element_type=jnp.float32).reshape(N_GX, N_GY, A_DEV, C)
    send_rows = jnp.concatenate([face_lists[:, :, 0], face_lists[:, :, 1], corner_lists[:, :, 0], corner_lists[:, :, 1]], axis=2).astype(jnp.int32)
    picked_proj = twice(lambda table, index: jnp.take(table, index, axis=0))(neigh_proj, send_rows)
    picked_pos = twice(lambda table, index: jnp.take(table, index, axis=1))(positions, send_rows)
    ghost_proj = to_holders(picked_proj, 2)
    ghost_pos = to_holders(picked_pos, 3) + ghost_offsets()[None, None]
    all_pos = jnp.concatenate([positions, ghost_pos], axis=3)
    all_proj = jnp.concatenate([neigh_proj, ghost_proj], axis=2)
    atom_flag = jnp.arange(A_DEV)[None, None, :] < domain_counts[:, :, None]
    atom_live = atom_flag.astype(jnp.float32)
    pair_live = ((jnp.arange(NBR)[None, None, :, None] < neighbour_counts[:, :, None, :]) & atom_flag[:, :, None, :]).astype(jnp.float32)
    flat_pos = all_pos.reshape(domains, 3, rows_all)
    flat_proj = all_proj.reshape(domains, rows_all, C)
    flat_center = center_proj.reshape(domains, A_DEV, C)
    flat_nbr = neighbours.reshape(domains, NBR, A_DEV)
    flat_live = pair_live.reshape(domains, NBR, A_DEV)

    def forward_one(item):
        return pair_terms(item[0], item[1], item[2], item[3], item[4], w_radial, w_latent)
    moments = lax.map(forward_one, (flat_pos, flat_proj, flat_center, flat_nbr, flat_live))
    moments = moments.reshape(N_GX, N_GY, rows_all, 9 * C)
    returned = to_owners(moments[:, :, A_DEV:, :], 2)
    own_moments = twice(lambda table, index, extra: table.at[index, :].add(extra))(moments[:, :, :A_DEV, :], send_rows, returned)

    def total_energy(values):
        return jnp.sum(twice(lambda vals, live: readout(vals, live, w_readout, w_energy))(values, atom_live))
    total, pull_total = jax.vjp(total_energy, own_moments)
    slope = pull_total(jnp.ones((), jnp.float32))[0]
    energy = total / jnp.sum(domain_counts.astype(jnp.float32))
    picked_slope = twice(lambda table, index: jnp.take(table, index, axis=0))(slope, send_rows)
    all_slope = jnp.concatenate([slope, to_holders(picked_slope, 2)], axis=2).reshape(domains, rows_all, 9 * C)

    def backward_one(item):
        unused, pull = jax.vjp(lambda placed: pair_terms(placed, item[1], item[2], item[3], item[4], w_radial, w_latent), item[0])
        return pull(item[5])[0]
    grads = lax.map(backward_one, (flat_pos, flat_proj, flat_center, flat_nbr, flat_live, all_slope))
    grads = grads.reshape(N_GX, N_GY, 3, rows_all)
    back_grads = to_owners(grads[:, :, :, A_DEV:], 3)
    own_grads = twice(lambda table, index, extra: table.at[:, index].add(extra))(grads[:, :, :, :A_DEV], send_rows, back_grads)
    return (energy, -own_grads)
```

```python
import functools
import math

import jax
import jax.numpy as jnp
from jax import lax
from jax.experimental import pallas as pl
from jax.experimental.pallas import tpu as pltpu
from jax.sharding import PartitionSpec as P

cutoff = 6.0
soften = 0.25
box_width = 4.0
f32 = jnp.float32
bf16 = jnp.bfloat16
MESH = pl.DeviceIdType.MESH

A = 128
C = 128
K = 32
GF = 64
GC = 16
NG = 2 * GF + 2 * GC
R = A + NG
NB = 8
PAIRS = K * A
STEP = 4
WIDE = STEP * A
ORDER = (0, 4, 5, 6, 7, 8, 1, 2, 3)
CHUNKS = ((0, 2), (2, 4), (4, 6), (6, 9))
GROUPS = ((0, GF), (GF, GF), (2 * GF, GC), (2 * GF + GC, GC))


def dot(a, b):
    return lax.dot_general(a, b, (((1,), (0,)), ((), ())), preferred_element_type=f32)


def dot_nt(a, b):
    return lax.dot_general(a, b, (((1,), (1,)), ((), ())), preferred_element_type=f32)


def split(x):
    hi = x.astype(bf16)
    lo = (x - hi.astype(f32)).astype(bf16)
    return hi, lo


def silu_parts(x):
    s = 0.5 + 0.5 * jnp.tanh(0.5 * x)
    y = x * s
    return y, s + y * (1.0 - s)


def pick_lanes(table, index):
    return jnp.take_along_axis(table, index, axis=1)


def kernel(
    sizes,
    feat_ref,
    pos_ref,
    nbr_ref,
    cnt_ref,
    dom_ref,
    face_ref,
    corner_ref,
    wc_ref,
    wn_ref,
    wr_ref,
    wl_ref,
    wo_ref,
    we_ref,
    energy_ref,
    force_ref,
    outf,
    outc,
    inf,
    inc,
    proj,
    left,
    cent,
    even,
    odd,
    brow,
    harm,
    geom,
    lat,
    d1s,
    d2s,
    term,
    mom,
    msend,
    mrecv,
    slope_send,
    slope_recv,
    gt,
    dw,
    dys,
    dbs,
    ddr,
    fsend,
    frecv,
    ebuf_a,
    ebuf_b,
    ebuf_c,
    s1,
    r1,
    s2,
    r2,
    s3,
    r3,
    s4,
    r4,
    sa,
    ra,
    sb,
    rb,
    sc,
    rc,
):
    nx, ny = sizes
    gx = lax.axis_index("gx")
    gy = lax.axis_index("gy")
    up_x, down_x = lax.rem(gx + 1, nx), lax.rem(gx + nx - 1, nx)
    up_y, down_y = lax.rem(gy + 1, ny), lax.rem(gy + ny - 1, ny)
    holders = ((down_x, gy), (gx, down_y), (down_x, down_y), (down_x, up_y))
    owners = ((up_x, gy), (gx, up_y), (up_x, up_y), (up_x, down_y))
    inner = min(nx, 8)
    outer = nx // inner
    block, place = gx // inner, lax.rem(gx, inner)

    def group_a(i):
        return (block * inner + i, gy)

    def group_b(i):
        return (i * inner + place, gy)

    def group_c(i):
        return (gx, i)

    stages = (
        (inner, place, group_a, ebuf_a, sa, ra),
        (outer, block, group_b, ebuf_b, sb, rb),
        (ny, gy, group_c, ebuf_c, sc, rc),
    )

    barrier = pltpu.get_barrier_semaphore()
    greeted = list(holders) + list(owners)
    for count, mine, where, unused_buf, unused_s, unused_r in stages:
        for s in range(1, count):
            greeted.append(where(lax.rem(mine + s, count)))
    for target in greeted:
        pl.semaphore_signal(barrier, inc=1, device_id=target, device_id_type=MESH)

    sub = lax.broadcasted_iota(jnp.int32, (A, A), 0)
    lane = lax.broadcasted_iota(jnp.int32, (A, A), 1)
    eye = jnp.where(sub == lane, 1.0, 0.0)
    lists_a = jnp.concatenate([face_ref[0:1, :], face_ref[1:2, :]], axis=1)
    none = jnp.full((1, A - 2 * GC), -1, jnp.int32)
    lists_b = jnp.concatenate([corner_ref[0:1, :], corner_ref[1:2, :], none], axis=1)
    pt_a = jnp.where(sub == lists_a, 1.0, 0.0)
    pt_b = jnp.where(sub == lists_b, 1.0, 0.0)
    pick = jnp.concatenate([pt_a.T, pt_b.T[0 : 2 * GC]], axis=0).astype(bf16)
    spread = jnp.concatenate([pt_a, pt_b], axis=1).astype(bf16)[:, 0:NG]
    feat = feat_ref[...]
    picked = dot(pick, feat)
    small = lax.broadcasted_iota(jnp.int32, (3, A), 0)
    wide = lax.broadcasted_iota(jnp.int32, (3, A), 1)
    pos = pos_ref[...]
    zero = jnp.zeros((3, A), f32)
    at_a = pick_lanes(pos, jnp.broadcast_to(lists_a, (3, A)))
    at_b = pick_lanes(pos, jnp.broadcast_to(jnp.maximum(lists_b, 0), (3, A)))
    at_a = at_a + jnp.where(small == jnp.where(wide < GF, 0, 1), box_width, zero)
    tilt = jnp.where(wide < GC, box_width, -box_width)
    at_b = at_b + jnp.where(small == 0, box_width, jnp.where(small == 1, tilt, zero))
    for g, (base, rows) in enumerate(GROUPS):
        buf, slot, at = (outf, g, at_a) if g < 2 else (outc, g - 2, at_b)
        buf[slot, 0:rows, :] = picked[base : base + rows]
        buf[slot, rows : rows + 8, :] = jnp.zeros((8, A), f32)
        buf[slot, rows : rows + 3, :] = at

    pl.semaphore_wait(barrier, len(greeted))

    def first_copy(g):
        src, dst, slot = (outf, inf, g) if g < 2 else (outc, inc, g - 2)
        return pltpu.make_async_remote_copy(
            src_ref=src.at[slot],
            dst_ref=dst.at[slot],
            send_sem=s1.at[g],
            recv_sem=r1.at[g],
            device_id=holders[g],
            device_id_type=MESH,
        )

    for g in (1, 3, 2, 0):
        first_copy(g).start()

    proj[0:A, :] = dot(feat, wn_ref[...])
    center = dot(feat, wc_ref[...])
    wr = wr_ref[...]
    wr_hi = wr.astype(bf16).astype(f32)
    proj[R : R + NB, :] = wr_hi
    proj[R + NB : R + 2 * NB, :] = wr_hi
    proj[R + 2 * NB : R + 3 * NB, :] = wr - wr_hi
    proj[R + 3 * NB :, :] = jnp.zeros((384 - R - 3 * NB, C), f32)
    own_t = proj[0:A, :].T.astype(bf16)
    left[:, 0:A] = own_t
    cent[...] = center.T - own_t.astype(f32)

    sub_g = lax.broadcasted_iota(jnp.int32, (NG, A), 0) + A

    def build(k, carry):
        lanes = pl.ds(pl.multiple_of(k * A, A), A)
        index = nbr_ref[pl.ds(k, 1), :]
        own = jnp.where(sub == index, 1.0, 0.0)
        even[0:A, lanes] = (eye + own).astype(bf16)
        odd[0:A, lanes] = (eye - own).astype(bf16)
        ghost = jnp.where(sub_g == index, 1.0, 0.0)
        even[A:R, lanes] = ghost.astype(bf16)
        odd[A:R, lanes] = (-ghost).astype(bf16)
        return carry

    lax.fori_loop(0, K, build, 0)

    for g in range(4):
        first_copy(g).wait_recv()
    for g, (base, rows) in enumerate(GROUPS):
        buf, slot = (inf, g) if g < 2 else (inc, g - 2)
        proj[A + base : A + base + rows, :] = dot(
            buf[slot, 0:rows, :].astype(bf16), wn_ref[...]
        )
    left[:, A : 2 * A] = proj[A : 2 * A, :].T.astype(bf16)
    left[:, 2 * A : 3 * A] = proj[2 * A : 3 * A, :].T.astype(bf16)
    ghost_a = jnp.where(wide < GF, inf[0, GF : GF + 3, :], inf[1, GF : GF + 3, :])
    ghost_b = jnp.where(wide < GC, inc[0, GC : GC + 3, :], inc[1, GC : GC + 3, :])

    nbr = nbr_ref[...]
    in_own = nbr < A
    in_face = nbr < 2 * A
    local = jnp.bitwise_and(nbr, A - 1)
    delta = []
    for c in range(3):
        tables = [
            jnp.broadcast_to(t[c : c + 1, :], (K, A)) for t in (pos, ghost_a, ghost_b)
        ]
        found = [pick_lanes(t, local) for t in tables]
        other = jnp.where(in_own, found[0], jnp.where(in_face, found[1], found[2]))
        delta.append(other - tables[0])
    dx, dy, dz = delta
    radius = jnp.sqrt(dx * dx + dy * dy + dz * dz + soften)
    inv = 1.0 / radius
    ux, uy, uz = dx * inv, dy * inv, dz * inv
    t = jnp.minimum(radius / cutoff, 1.0)
    t2 = t * t
    t5 = t2 * t2 * t
    t6 = t5 * t
    envelope = 1.0 + t6 * (-28.0 + t * (48.0 - 21.0 * t))
    slot_no = lax.broadcasted_iota(jnp.int32, (K, A), 0)
    atom_no = lax.broadcasted_iota(jnp.int32, (K, A), 1)
    alive = jnp.logical_and(slot_no < cnt_ref[...], atom_no < dom_ref[...])
    live = jnp.where(alive, 1.0, 0.0)
    root3, root5, root15 = math.sqrt(3.0), math.sqrt(5.0), math.sqrt(15.0)
    y_all = (
        None,
        root3 * ux,
        root3 * uy,
        root3 * uz,
        root15 * ux * uy,
        root15 * uy * uz,
        0.5 * root5 * (3.0 * uz * uz - 1.0),
        root15 * ux * uz,
        0.5 * root15 * (ux * ux - uy * uy),
    )
    for q, m in enumerate(ORDER):
        if m:
            harm[q] = y_all[m]
    geom[0] = envelope * live
    geom[1] = live * (t5 * (-168.0 + t * (336.0 - 168.0 * t)) * jnp.where(radius < cutoff, 1.0 / cutoff, 0.0))
    geom[2], geom[3], geom[4], geom[5] = inv, ux, uy, uz
    theta = radius * (math.pi / cutoff)
    sin1, cos1 = jnp.sin(theta), jnp.cos(theta)
    norm = math.sqrt(2.0 / cutoff)
    s_old, s_now = jnp.zeros_like(theta), sin1
    c_old, c_now = jnp.ones_like(theta), cos1
    for n in range(1, NB + 1):
        value = norm * s_now * inv
        brow[pl.ds(n - 1, K, stride=NB), :] = value
        geom[5 + n] = norm * (n * math.pi / cutoff) * c_now * inv - value * inv
        s_old, s_now = s_now, 2.0 * cos1 * s_now - s_old
        c_old, c_now = c_now, 2.0 * cos1 * c_now - c_old

    def put_basis(k, carry):
        lanes = pl.ds(pl.multiple_of(k * A, A), A)
        tile = brow[pl.ds(pl.multiple_of(k * NB, NB), NB), :]
        hi = tile.astype(bf16).astype(f32)
        rows = jnp.concatenate([hi, tile - hi, hi, jnp.zeros_like(hi)], axis=0)
        even[R : R + 4 * NB, lanes] = rows.astype(bf16)
        return carry

    lax.fori_loop(0, K, put_basis, 0)

    wl_t = wl_ref[...].astype(f32).T.astype(bf16)
    cent_wide = jnp.concatenate([cent[...]] * STEP, axis=1)

    def forward(q, carry):
        lanes = pl.ds(pl.multiple_of(q * WIDE, WIDE), WIDE)
        pre = dot(left[:, 0 : R + 4 * NB], even[:, lanes]) + cent_wide
        hidden, d1 = silu_parts(pre)
        d1s[:, lanes] = d1
        latent, d2 = silu_parts(dot(wl_t, hidden.astype(bf16)))
        lat[:, lanes] = latent
        d2s[:, lanes] = d2
        for s in range(STEP):
            k = q * STEP + s
            cols = pl.ds(pl.multiple_of(k * A, A), A)
            w = latent[:, s * A : (s + 1) * A] * geom[0, pl.ds(k, 1), :]
            for at, m in enumerate(ORDER):
                value = w * harm[at, pl.ds(k, 1), :] if m else w
                term[at * C : (at + 1) * C, cols] = value.astype(bf16)
        return carry

    lax.fori_loop(0, K // STEP, forward, 0)

    def group_copy(src, dst, send, recv, g, part, targets):
        base, rows = GROUPS[g]
        first, last = CHUNKS[part]
        view = (pl.ds(base, rows), pl.ds(first * C, (last - first) * C))
        sem = part * 4 + g
        return pltpu.make_async_remote_copy(
            src_ref=src.at[view],
            dst_ref=dst.at[view],
            send_sem=send.at[sem],
            recv_sem=recv.at[sem],
            device_id=targets[g],
            device_id_type=MESH,
        )

    def moment_copy(g, part):
        return group_copy(msend, mrecv, s2, r2, g, part, owners)

    def slope_copy(g, part):
        return group_copy(slope_send, slope_recv, s3, r3, g, part, holders)

    for part, (first, last) in enumerate(CHUNKS):
        cols = slice(first * C, last * C)
        side = even if first < 6 else odd
        found = dot_nt(side[0:R, :], term[cols, :])
        mom[:, cols] = found[0:A]
        msend[:, cols] = found[A:R]
        for g in (1, 3, 2, 0):
            moment_copy(g, part).start()

    spread2 = jnp.concatenate([spread, spread], axis=1)
    for part, (first, last) in enumerate(CHUNKS):
        cols = slice(first * C, last * C)
        for g in range(4):
            moment_copy(g, part).wait_recv()
        hi, lo = split(mrecv[:, cols])
        mom[:, cols] = mom[:, cols] + dot(spread2, jnp.concatenate([hi, lo], axis=0))

    levels = ((0, 1), (6, 9), (1, 6))
    sums = []
    for first, last in levels:
        total = None
        for at in range(first, last):
            value = mom[:, at * C : (at + 1) * C]
            total = value * value if total is None else total + value * value
        sums.append(total)
    packed = jnp.concatenate([jnp.log1p(x) for x in sums], axis=1).astype(bf16)
    inner_act = dot(packed, wo_ref[...])
    act, d_act = silu_parts(inner_act)
    row_live = jnp.where(sub < dom_ref[...], 1.0, 0.0)
    weighted = row_live * we_ref[...]
    own_energy = jnp.sum(jnp.sum(act * weighted, axis=0, keepdims=True), axis=1, keepdims=True)
    d_inv = dot_nt((d_act * weighted).astype(bf16), wo_ref[...]).astype(bf16).astype(f32)
    pick2 = jnp.concatenate([pick, pick], axis=1)
    scale = [2.0 * d_inv[:, i * C : (i + 1) * C] / (1.0 + sums[i]) for i in range(3)]
    which = (0, 2, 2, 2, 2, 2, 1, 1, 1)
    for part, (first, last) in enumerate(CHUNKS):
        for at in range(first, last):
            cols = slice(at * C, (at + 1) * C)
            value = mom[:, cols] * scale[which[at]]
            hi, lo = split(value)
            slope_send[:, cols] = dot(pick2, jnp.concatenate([hi, lo], axis=0))
            gt[cols, 0:A] = value.T.astype(bf16)
        for g in (1, 3, 2, 0):
            slope_copy(g, part).start()

    def stage_copy(stage, peer, slot):
        count, mine, where, buf, send, recv = stages[stage]
        return pltpu.make_async_remote_copy(
            src_ref=buf.at[mine],
            dst_ref=buf.at[slot],
            send_sem=send.at[peer],
            recv_sem=recv.at[slot],
            device_id=where(peer),
            device_id_type=MESH,
        )

    def stage_start(stage, value):
        count, mine, where, buf, send, recv = stages[stage]
        buf[mine] = value
        for s in range(1, count):
            stage_copy(stage, lax.rem(mine + s, count), mine).start()

    def stage_end(stage):
        count, mine, where, buf, send, recv = stages[stage]
        for s in range(1, count):
            peer = lax.rem(mine + s, count)
            stage_copy(stage, peer, peer).wait_recv()
        total = buf[0]
        for i in range(1, count):
            total = total + buf[i]
        return total

    half = lax.broadcasted_iota(jnp.int32, (8, C), 0)
    pair = jnp.where(half == 0, own_energy, dom_ref[...].astype(f32))
    stage_start(0, pair)

    def pull(q, lo_row, hi_row):
        lanes = pl.ds(pl.multiple_of(q * WIDE, WIDE), WIDE)
        at_even = dot(gt[0 : 6 * C, lo_row:hi_row], even[lo_row:hi_row, lanes])
        at_odd = dot(gt[6 * C : 9 * C, lo_row:hi_row], odd[lo_row:hi_row, lanes])
        outs = []
        for s in range(STEP):
            k = q * STEP + s
            cols = pl.ds(pl.multiple_of(k * A, A), A)
            w = lat[:, cols] * geom[0, pl.ds(k, 1), :]
            total = None
            rows = []
            for at, m in enumerate(ORDER):
                part = at_even if at < 6 else at_odd
                base = (at if at < 6 else at - 6) * C
                h = part[base : base + C, s * A : (s + 1) * A]
                if m:
                    rows.append(jnp.sum(h * w, axis=0, keepdims=True))
                    total = total + h * harm[at, pl.ds(k, 1), :]
                else:
                    total = h
            outs.append((total, rows))
        return outs

    def pull_own(q, carry):
        for s, (total, rows) in enumerate(pull(q, 0, A)):
            k = q * STEP + s
            dw[:, pl.ds(pl.multiple_of(k * A, A), A)] = total
            for at, row in enumerate(rows):
                dys[pl.ds(k * 16 + at, 1), :] = row
        return carry

    lax.fori_loop(0, K // STEP, pull_own, 0)
    stage_start(1, stage_end(0))

    for part, (first, last) in enumerate(CHUNKS):
        for g in range(4):
            slope_copy(g, part).wait_recv()
        for at in range(first, last):
            cols = slice(at * C, (at + 1) * C)
            gt[cols, A : 2 * A] = slope_recv[0:A, cols].T.astype(bf16)
            gt[cols, 2 * A : R] = slope_recv[A:NG, cols].T.astype(bf16)

    wl = wl_ref[...]
    wr2 = jnp.concatenate([wr_hi, wr - wr_hi], axis=0).astype(bf16)

    def pull_ghost(q, carry):
        for s, (total, rows) in enumerate(pull(q, A, R)):
            k = q * STEP + s
            cols = pl.ds(pl.multiple_of(k * A, A), A)
            d_w = dw[:, cols] + total
            for at, row in enumerate(rows):
                spot = pl.ds(k * 16 + at, 1)
                dys[spot, :] = dys[spot, :] + row
            dys[pl.ds(k * 16 + 8, 1), :] = jnp.sum(d_w * lat[:, cols], axis=0, keepdims=True)
            d_pre2 = d_w * geom[0, pl.ds(k, 1), :] * d2s[:, cols]
            d_hidden = dot(wl, d_pre2.astype(bf16)).astype(bf16).astype(f32)
            hi, lo = split(d_hidden * d1s[:, cols])
            two = dot(wr2, hi)
            d_basis = two[0:NB] + two[NB : 2 * NB] + dot(wr2[0:NB], lo)
            dbs[pl.ds(pl.multiple_of(k * NB, NB), NB), :] = d_basis
        return carry

    lax.fori_loop(0, K // STEP, pull_ghost, 0)
    stage_start(2, stage_end(1))

    g_of = {m: dys[pl.ds(at - 1, K, stride=16), :] for at, m in enumerate(ORDER) if m}
    d_radius = dys[pl.ds(8, K, stride=16), :] * geom[1]
    for n in range(1, NB + 1):
        d_radius = d_radius + dbs[pl.ds(n - 1, K, stride=NB), :] * geom[5 + n]
    inv, ux, uy, uz = geom[2], geom[3], geom[4], geom[5]
    dux = root3 * g_of[1] + root15 * (uy * g_of[4] + uz * g_of[7] + ux * g_of[8])
    duy = root3 * g_of[2] + root15 * (ux * g_of[4] + uz * g_of[5] - uy * g_of[8])
    duz = root3 * g_of[3] + root15 * (uy * g_of[5] + ux * g_of[7]) + 3.0 * root5 * uz * g_of[6]
    along = d_radius - (dux * ux + duy * uy + duz * uz) * inv
    for c, (du, u) in enumerate(((dux, ux), (duy, uy), (duz, uz))):
        value = du * inv + u * along
        hi = value.astype(bf16).astype(f32)
        brow[pl.ds(c, K, stride=NB), :] = hi
        brow[pl.ds(c + 3, K, stride=NB), :] = value - hi
    brow[pl.ds(6, K, stride=NB), :] = jnp.zeros((K, A), f32)
    brow[pl.ds(7, K, stride=NB), :] = jnp.zeros((K, A), f32)
    for k in range(K):
        ddr[:, k * A : (k + 1) * A] = brow[k * NB : (k + 1) * NB, :].astype(bf16)
    found = dot_nt(odd[0:R, :], ddr[...])
    wide_found = jnp.concatenate([found, jnp.zeros((R, A - 8), f32)], axis=1)
    full = jnp.concatenate([wide_found, jnp.zeros((3 * A - R, A), f32)], axis=0)
    flipped = [full[i * A : (i + 1) * A].T[0:8] for i in range(3)]
    fsend[0] = flipped[1]
    fsend[1] = flipped[2]

    def force_copy(g):
        return pltpu.make_async_remote_copy(
            src_ref=fsend.at[g // 2],
            dst_ref=frecv.at[g],
            send_sem=s4.at[g],
            recv_sem=r4.at[g],
            device_id=owners[g],
            device_id_type=MESH,
        )

    for g in (1, 3, 2, 0):
        force_copy(g).start()
    for g in range(4):
        force_copy(g).wait_recv()
    wide8 = lax.broadcasted_iota(jnp.int32, (8, A), 1)
    back_a = jnp.where(wide8 < GF, frecv[0], frecv[1])
    back_b = jnp.where(wide8 < GC, frecv[2], frecv[3])
    back = jnp.concatenate([back_a, back_b[:, 0 : 2 * GC]], axis=1)
    back = back + 0.0
    hi, lo = split(back)
    total = flipped[0] + dot(hi, pick) + dot(lo, pick)
    force_ref[...] = total[0:3] + total[3:6]

    sums = stage_end(2)
    energy_ref[...] = sums[0:1, 0:1] / sums[1:2, 0:1]

    for g in range(4):
        first_copy(g).wait_send()
        force_copy(g).wait_send()
        for part in range(len(CHUNKS)):
            moment_copy(g, part).wait_send()
            slope_copy(g, part).wait_send()
    for stage, (count, mine, where, buf, send, recv) in enumerate(stages):
        for s in range(1, count):
            stage_copy(stage, lax.rem(mine + s, count), mine).wait_send()


def on_device(
    sizes,
    features,
    positions,
    neighbours,
    neighbour_counts,
    domain_counts,
    face_lists,
    corner_lists,
    w_center,
    w_neigh,
    w_radial,
    w_latent,
    w_readout,
    w_energy,
):
    nx, ny = sizes
    inner = min(nx, 8)
    outer = nx // inner
    vmem = pltpu.VMEM
    dma = pltpu.SemaphoreType.DMA
    scratch = [
        vmem((2, GF + 8, C), f32),
        vmem((2, GC + 8, C), f32),
        vmem((2, GF + 8, C), f32),
        vmem((2, GC + 8, C), f32),
        vmem((3 * A, C), f32),
        vmem((C, 3 * A), bf16),
        vmem((C, A), f32),
        vmem((R + 4 * NB, PAIRS), bf16),
        vmem((R, PAIRS), bf16),
        vmem((K * NB, A), f32),
        vmem((9, K, A), f32),
        vmem((6 + NB, K, A), f32),
        vmem((C, PAIRS), f32),
        vmem((C, PAIRS), f32),
        vmem((C, PAIRS), f32),
        vmem((9 * C, PAIRS), bf16),
        vmem((A, 9 * C), f32),
        vmem((NG, 9 * C), f32),
        vmem((NG, 9 * C), f32),
        vmem((NG, 9 * C), f32),
        vmem((NG, 9 * C), f32),
        vmem((9 * C, R), bf16),
        vmem((C, PAIRS), f32),
        vmem((K * 16, A), f32),
        vmem((K * NB, A), f32),
        vmem((8, PAIRS), bf16),
        vmem((2, 8, A), f32),
        vmem((4, 8, A), f32),
        vmem((inner, 8, C), f32),
        vmem((outer, 8, C), f32),
        vmem((ny, 8, C), f32),
        dma((4,)),
        dma((4,)),
        dma((16,)),
        dma((16,)),
        dma((16,)),
        dma((16,)),
        dma((4,)),
        dma((4,)),
        dma((inner,)),
        dma((inner,)),
        dma((outer,)),
        dma((outer,)),
        dma((ny,)),
        dma((ny,)),
    ]
    energy, forces = pl.pallas_call(
        functools.partial(kernel, sizes),
        out_shape=(
            jax.ShapeDtypeStruct((1, 1), f32),
            jax.ShapeDtypeStruct((3, A), f32),
        ),
        in_specs=[pl.BlockSpec(memory_space=pltpu.VMEM)] * 13,
        out_specs=(
            pl.BlockSpec(memory_space=pltpu.VMEM),
            pl.BlockSpec(memory_space=pltpu.VMEM),
        ),
        scratch_shapes=scratch,
        compiler_params=pltpu.CompilerParams(
            collective_id=0, has_side_effects=True, vmem_limit_bytes=50 * 1024 * 1024
        ),
    )(
        features[0, 0],
        positions[0, 0],
        neighbours[0, 0],
        neighbour_counts[0],
        domain_counts,
        face_lists[0, 0],
        corner_lists[0, 0],
        w_center,
        w_neigh,
        w_radial,
        w_latent,
        w_readout,
        w_energy[None, :],
    )
    return (energy.reshape(()), forces[None, None])


def solution(mesh):
    sizes = (mesh.shape["gx"], mesh.shape["gy"])
    placed = (
        P("gx", "gy", None, None),
        P("gx", "gy", None, None),
        P("gx", "gy", None, None),
        P("gx", "gy", None),
        P("gx", "gy"),
        P("gx", "gy", None, None),
        P("gx", "gy", None, None),
        P(),
        P(),
        P(),
        P(),
        P(),
        P(),
    )
    return jax.shard_map(
        functools.partial(on_device, sizes),
        mesh=mesh,
        in_specs=placed,
        out_specs=(P(), P("gx", "gy", None, None)),
        check_vma=False,
    )
```

```python
import functools
import math

import jax
import jax.numpy as jnp
from jax import lax
from jax.experimental import pallas as pl
from jax.experimental.pallas import tpu as pltpu
from jax.sharding import PartitionSpec as P

cutoff = 6.0
soften = 0.25
box_width = 4.0
f32 = jnp.float32
bf16 = jnp.bfloat16
MESH = pl.DeviceIdType.MESH

A = 128
C = 128
K = 32
GF = 64
GC = 16
NG = 2 * GF + 2 * GC
R = A + NG
NB = 8
PAIRS = K * A
STEP = 4
WIDE = STEP * A
ORDER = (0, 4, 5, 6, 7, 8, 1, 2, 3)
MOMENT_PARTS = ((0, 2), (2, 4), (4, 6), (6, 9))
SLOPE_PARTS = ((6, 7), (7, 9), (4, 6), (2, 4), (1, 2), (0, 1))
GROUPS = ((0, GF), (GF, GF), (2 * GF, GC), (2 * GF + GC, GC))


def dot(a, b):
    return lax.dot_general(a, b, (((1,), (0,)), ((), ())), preferred_element_type=f32)


def dot_nt(a, b):
    return lax.dot_general(a, b, (((1,), (1,)), ((), ())), preferred_element_type=f32)


def split(x):
    hi = x.astype(bf16)
    lo = (x - hi.astype(f32)).astype(bf16)
    return hi, lo


def silu_parts(x):
    s = 0.5 + 0.5 * jnp.tanh(0.5 * x)
    y = x * s
    return y, s + y * (1.0 - s)


def pick_lanes(table, index):
    return jnp.take_along_axis(table, index, axis=1)


def kernel(
    sizes,
    feat_hbm,
    pos_hbm,
    nbr_hbm,
    cnt_hbm,
    dom_hbm,
    face_hbm,
    corner_hbm,
    wc_hbm,
    wn_hbm,
    wr_hbm,
    wl_hbm,
    wo_hbm,
    we_hbm,
    energy_ref,
    force_ref,
    feat_ref,
    pos_ref,
    nbr_ref,
    cnt_ref,
    dom_ref,
    face_ref,
    corner_ref,
    wc_ref,
    wn_ref,
    wr_ref,
    wl_ref,
    wo_ref,
    we_ref,
    load_sem,
    force_out,
    energy_out,
    out_sem,
    outf,
    outc,
    inf,
    inc,
    proj,
    left,
    cent,
    even,
    odd,
    brow,
    drow,
    slow,
    harm,
    tiles,
    geom,
    pres,
    acts,
    term,
    mom,
    halves,
    msend,
    mrecv,
    slope_send,
    slope_recv,
    gt,
    ays,
    bys,
    ddr,
    fsend,
    frecv,
    ebuf_a,
    ebuf_b,
    ebuf_c,
    s1,
    r1,
    s2,
    r2,
    s3,
    r3,
    s4,
    r4,
    sa,
    ra,
    sb,
    rb,
    sc,
    rc,
):
    nx, ny = sizes
    gx = lax.axis_index("gx")
    gy = lax.axis_index("gy")
    up_x, down_x = lax.rem(gx + 1, nx), lax.rem(gx + nx - 1, nx)
    up_y, down_y = lax.rem(gy + 1, ny), lax.rem(gy + ny - 1, ny)
    holders = ((down_x, gy), (gx, down_y), (down_x, down_y), (down_x, up_y))
    owners = ((up_x, gy), (gx, up_y), (up_x, up_y), (up_x, down_y))
    inner = min(nx, 8)
    outer = nx // inner
    block, place = gx // inner, lax.rem(gx, inner)

    def group_a(i):
        return (block * inner + i, gy)

    def group_b(i):
        return (i * inner + place, gy)

    def group_c(i):
        return (gx, i)

    stages = (
        (inner, place, group_a, ebuf_a, sa, ra),
        (outer, block, group_b, ebuf_b, sb, rb),
        (ny, gy, group_c, ebuf_c, sc, rc),
    )

    barrier = pltpu.get_barrier_semaphore()
    greeted = list(holders) + list(owners)
    for count, mine, where, unused_buf, unused_s, unused_r in stages:
        for s in range(1, count):
            greeted.append(where(lax.rem(mine + s, count)))
    for target in greeted:
        pl.semaphore_signal(barrier, inc=1, device_id=target, device_id_type=MESH)

    first_loads = [
        (face_hbm, face_ref),
        (corner_hbm, corner_ref),
        (feat_hbm, feat_ref),
        (pos_hbm, pos_ref),
    ]
    later_loads = [
        (nbr_hbm, nbr_ref),
        (wn_hbm, wn_ref),
        (wc_hbm, wc_ref),
        (wr_hbm, wr_ref),
        (cnt_hbm, cnt_ref),
        (dom_hbm, dom_ref),
        (wl_hbm, wl_ref),
        (wo_hbm, wo_ref),
        (we_hbm, we_ref),
    ]
    loads = [
        pltpu.make_async_copy(src, dst, load_sem.at[i])
        for i, (src, dst) in enumerate(first_loads + later_loads)
    ]
    for load in loads:
        load.start()
    for load in loads[: len(first_loads)]:
        load.wait()

    sub = lax.broadcasted_iota(jnp.int32, (A, A), 0)
    lane = lax.broadcasted_iota(jnp.int32, (A, A), 1)
    eye = jnp.where(sub == lane, 1.0, 0.0)
    lists_a = jnp.concatenate([face_ref[0:1, :], face_ref[1:2, :]], axis=1)
    none = jnp.full((1, A - 2 * GC), -1, jnp.int32)
    lists_b = jnp.concatenate([corner_ref[0:1, :], corner_ref[1:2, :], none], axis=1)
    pt_a = jnp.where(sub == lists_a, 1.0, 0.0)
    pt_b = jnp.where(sub == lists_b, 1.0, 0.0)
    pick = jnp.concatenate([pt_a.T, pt_b.T[0 : 2 * GC]], axis=0).astype(bf16)
    spread = jnp.concatenate([pt_a, pt_b], axis=1).astype(bf16)[:, 0:NG]
    feat = feat_ref[...]
    picked = dot(pick, feat)
    small = lax.broadcasted_iota(jnp.int32, (3, A), 0)
    wide = lax.broadcasted_iota(jnp.int32, (3, A), 1)
    pos = jnp.concatenate([pos_ref[c] for c in range(3)], axis=0)
    zero = jnp.zeros((3, A), f32)
    at_a = pick_lanes(pos, jnp.broadcast_to(lists_a, (3, A)))
    at_b = pick_lanes(pos, jnp.broadcast_to(jnp.maximum(lists_b, 0), (3, A)))
    at_a = at_a + jnp.where(small == jnp.where(wide < GF, 0, 1), box_width, zero)
    tilt = jnp.where(wide < GC, box_width, -box_width)
    at_b = at_b + jnp.where(small == 0, box_width, jnp.where(small == 1, tilt, zero))
    for g, (base, rows) in enumerate(GROUPS):
        buf, slot, at = (outf, g, at_a) if g < 2 else (outc, g - 2, at_b)
        buf[slot, 0:rows, :] = picked[base : base + rows]
        buf[slot, rows : rows + 8, :] = jnp.zeros((8, A), f32)
        buf[slot, rows : rows + 3, :] = at

    pl.semaphore_wait(barrier, len(greeted))

    def wait_bytes(ref, sem):
        pltpu.make_async_copy(ref, ref, sem).wait()

    def first_copy(g):
        src, dst, slot = (outf, inf, g) if g < 2 else (outc, inc, g - 2)
        return pltpu.make_async_remote_copy(
            src_ref=src.at[slot],
            dst_ref=dst.at[slot],
            send_sem=s1.at[g // 2],
            recv_sem=r1.at[g // 2],
            device_id=holders[g],
            device_id_type=MESH,
        )

    for g in (1, 3, 2, 0):
        first_copy(g).start()

    for load in loads[len(first_loads) :]:
        load.wait()

    proj[0:A, :] = dot(feat, wn_ref[...])
    center = dot(feat, wc_ref[...])
    wr = wr_ref[...]
    wr_hi = wr.astype(bf16).astype(f32)
    proj[R : R + NB, :] = wr_hi
    proj[R + NB : R + 2 * NB, :] = wr_hi
    proj[R + 2 * NB : R + 3 * NB, :] = wr - wr_hi
    proj[R + 3 * NB :, :] = jnp.zeros((384 - R - 3 * NB, C), f32)
    own_t = proj[0:A, :].T.astype(bf16)
    left[:, 0:A] = own_t
    cent[...] = center.T - own_t.astype(f32)

    sub_g = lax.broadcasted_iota(jnp.int32, (NG, A), 0) + A

    def build(k, carry):
        lanes = pl.ds(pl.multiple_of(k * A, A), A)
        index = nbr_ref[pl.ds(k, 1), :]
        own = jnp.where(sub == index, 1.0, 0.0)
        even[0:A, lanes] = (eye + own).astype(bf16)
        odd[0:A, lanes] = (eye - own).astype(bf16)
        ghost = jnp.where(sub_g == index, 1.0, 0.0)
        even[A:R, lanes] = ghost.astype(bf16)
        odd[A:R, lanes] = (-ghost).astype(bf16)
        return carry

    lax.fori_loop(0, K, build, 0)

    wait_bytes(inf, r1.at[0])
    wait_bytes(inc, r1.at[1])
    for g, (base, rows) in enumerate(GROUPS):
        buf, slot = (inf, g) if g < 2 else (inc, g - 2)
        proj[A + base : A + base + rows, :] = dot(
            buf[slot, 0:rows, :].astype(bf16), wn_ref[...]
        )
    left[:, A : 2 * A] = proj[A : 2 * A, :].T.astype(bf16)
    left[:, 2 * A : 3 * A] = proj[2 * A : 3 * A, :].T.astype(bf16)
    ghost_a = jnp.where(wide < GF, inf[0, GF : GF + 3, :], inf[1, GF : GF + 3, :])
    ghost_b = jnp.where(wide < GC, inc[0, GC : GC + 3, :], inc[1, GC : GC + 3, :])

    nbr = nbr_ref[...]
    in_own = nbr < A
    in_face = nbr < 2 * A
    local = jnp.bitwise_and(nbr, A - 1)
    delta = []
    for c in range(3):
        tables = [
            jnp.broadcast_to(t[c : c + 1, :], (K, A)) for t in (pos, ghost_a, ghost_b)
        ]
        found = [pick_lanes(t, local) for t in tables]
        other = jnp.where(in_own, found[0], jnp.where(in_face, found[1], found[2]))
        delta.append(other - tables[0])
    dx, dy, dz = delta
    radius = jnp.sqrt(dx * dx + dy * dy + dz * dz + soften)
    inv = 1.0 / radius
    ux, uy, uz = dx * inv, dy * inv, dz * inv
    t = jnp.minimum(radius / cutoff, 1.0)
    t2 = t * t
    t5 = t2 * t2 * t
    t6 = t5 * t
    envelope = 1.0 + t6 * (-28.0 + t * (48.0 - 21.0 * t))
    slot_no = lax.broadcasted_iota(jnp.int32, (K, A), 0)
    atom_no = lax.broadcasted_iota(jnp.int32, (K, A), 1)
    alive = jnp.logical_and(slot_no < cnt_ref[...], atom_no < dom_ref[...])
    live = jnp.where(alive, 1.0, 0.0)
    root3, root5, root15 = math.sqrt(3.0), math.sqrt(5.0), math.sqrt(15.0)
    y_all = (
        None,
        root3 * ux,
        root3 * uy,
        root3 * uz,
        root15 * ux * uy,
        root15 * uy * uz,
        0.5 * root5 * (3.0 * uz * uz - 1.0),
        root15 * ux * uz,
        0.5 * root15 * (ux * ux - uy * uy),
    )
    for q, m in enumerate(ORDER):
        if m:
            harm[q] = y_all[m]
    geom[0] = envelope * live
    geom[1] = live * (t5 * (-168.0 + t * (336.0 - 168.0 * t)) * jnp.where(radius < cutoff, 1.0 / cutoff, 0.0))
    geom[2], geom[3], geom[4], geom[5] = inv, ux, uy, uz
    theta = radius * (math.pi / cutoff)
    sin1, cos1 = jnp.sin(theta), jnp.cos(theta)
    norm = math.sqrt(2.0 / cutoff)
    s_old, s_now = jnp.zeros_like(theta), sin1
    c_old, c_now = jnp.ones_like(theta), cos1
    for n in range(1, NB + 1):
        value = norm * s_now * inv
        brow[pl.ds(n - 1, K, stride=NB), :] = value
        drow[pl.ds(n - 1, K, stride=NB), :] = (
            norm * (n * math.pi / cutoff) * c_now * inv - value * inv
        )
        s_old, s_now = s_now, 2.0 * cos1 * s_now - s_old
        c_old, c_now = c_now, 2.0 * cos1 * c_now - c_old

    def put_basis(k, carry):
        lanes = pl.ds(pl.multiple_of(k * A, A), A)
        tile = brow[pl.ds(pl.multiple_of(k * NB, NB), NB), :]
        hi = tile.astype(bf16).astype(f32)
        rows = jnp.concatenate([hi, tile - hi, hi, jnp.zeros_like(hi)], axis=0)
        even[R : R + 4 * NB, lanes] = rows.astype(bf16)
        tile = drow[pl.ds(pl.multiple_of(k * NB, NB), NB), :]
        hi = tile.astype(bf16).astype(f32)
        rows = jnp.concatenate([hi, tile - hi, hi, jnp.zeros_like(hi)], axis=0)
        slow[:, lanes] = rows.astype(bf16)
        for at in range(1, 9):
            row = jnp.broadcast_to(harm[at, pl.ds(k, 1), :], (16, A))
            tiles[at, pl.ds(k, 1)] = row.astype(bf16)[None]
        return carry

    lax.fori_loop(0, K, put_basis, 0)

    wl_t = wl_ref[...].astype(f32).T.astype(bf16)
    cent_wide = jnp.concatenate([cent[...]] * STEP, axis=1)

    def forward(q, carry):
        lanes = pl.ds(pl.multiple_of(q * WIDE, WIDE), WIDE)
        pre = dot(left[:, 0 : R + 4 * NB], even[:, lanes]) + cent_wide
        pres[:, lanes] = pre
        hidden = pre * (0.5 + 0.5 * jnp.tanh(0.5 * pre))
        act = dot(wl_t, hidden.astype(bf16))
        acts[:, lanes] = act
        latent = act * (0.5 + 0.5 * jnp.tanh(0.5 * act))
        for s in range(STEP):
            k = q * STEP + s
            cols = pl.ds(pl.multiple_of(k * A, A), A)
            w = latent[:, s * A : (s + 1) * A] * geom[0, pl.ds(k, 1), :]
            term[0:C, cols] = w.astype(bf16)
        return carry

    lax.fori_loop(0, K // STEP, forward, 0, unroll=8)

    def group_copy(src, dst, send, recv, g, part, targets, parts):
        base, rows = GROUPS[g]
        first, last = parts[part]
        view = (pl.ds(base, rows), pl.ds(first * C, (last - first) * C))
        return pltpu.make_async_remote_copy(
            src_ref=src.at[view],
            dst_ref=dst.at[view],
            send_sem=send.at[part],
            recv_sem=recv.at[part],
            device_id=targets[g],
            device_id_type=MESH,
        )

    def wait_part(ref, sem, parts, part):
        first, last = parts[part]
        wait_bytes(ref.at[:, pl.ds(first * C, (last - first) * C)], sem.at[part])

    def moment_copy(g, part):
        return group_copy(msend, mrecv, s2, r2, g, part, owners, MOMENT_PARTS)

    def slope_copy(g, part):
        return group_copy(slope_send, slope_recv, s3, r3, g, part, holders, SLOPE_PARTS)

    def build_terms(first, last):
        for at in range(max(first, 1), last):
            for k in range(K):
                cols = slice(k * A, (k + 1) * A)
                tile = jnp.concatenate([tiles[at, k]] * (C // 16), axis=0)
                term[at * C : (at + 1) * C, cols] = term[0:C, cols] * tile

    build_terms(*MOMENT_PARTS[0])
    for part, (first, last) in enumerate(MOMENT_PARTS):
        if part + 1 < len(MOMENT_PARTS):
            build_terms(*MOMENT_PARTS[part + 1])
        cols = slice(first * C, last * C)
        side = even if first < 6 else odd
        half = PAIRS // 2
        size = (last - first) * C
        halves[0, :, 0:size] = dot_nt(side[0:R, 0:half], term[cols, 0:half])
        halves[1, :, 0:size] = dot_nt(side[0:R, half:], term[cols, half:])
        mom[:, cols] = halves[0, 0:A, 0:size] + halves[1, 0:A, 0:size]
        msend[:, cols] = halves[0, A:R, 0:size] + halves[1, A:R, 0:size]
        for g in (1, 3, 2, 0):
            moment_copy(g, part).start()

    def slope_of_latents(q, carry):
        lanes = pl.ds(pl.multiple_of(q * WIDE, WIDE), WIDE)
        unused_hidden, d1 = silu_parts(pres[:, lanes])
        d_hidden = d1 * dot(left[:, R : R + 4 * NB], slow[:, lanes])
        latent, d2 = silu_parts(acts[:, lanes])
        d_latent = d2 * dot(wl_t, d_hidden.astype(bf16))
        for s in range(STEP):
            k = q * STEP + s
            cols = pl.ds(pl.multiple_of(k * A, A), A)
            here = slice(s * A, (s + 1) * A)
            env, d_env = geom[0, pl.ds(k, 1), :], geom[1, pl.ds(k, 1), :]
            pres[:, cols] = latent[:, here] * env
            acts[:, cols] = d_latent[:, here] * env + latent[:, here] * d_env
        return carry

    lax.fori_loop(0, K // STEP, slope_of_latents, 0, unroll=2)

    spread2 = jnp.concatenate([spread, spread], axis=1)
    for part, (first, last) in enumerate(MOMENT_PARTS):
        cols = slice(first * C, last * C)
        wait_part(mrecv, r2, MOMENT_PARTS, part)
        hi, lo = split(mrecv[:, cols])
        mom[:, cols] = mom[:, cols] + dot(spread2, jnp.concatenate([hi, lo], axis=0))

    levels = ((0, 1), (6, 9), (1, 6))
    sums = []
    for first, last in levels:
        total = None
        for at in range(first, last):
            value = mom[:, at * C : (at + 1) * C]
            total = value * value if total is None else total + value * value
        sums.append(total)
    packed = jnp.concatenate([jnp.log1p(x) for x in sums], axis=1).astype(bf16)
    inner_act = dot(packed, wo_ref[...])
    act, d_act = silu_parts(inner_act)
    row_live = jnp.where(sub < dom_ref[...], 1.0, 0.0)
    weighted = row_live * we_ref[...]
    own_energy = jnp.sum(jnp.sum(act * weighted, axis=0, keepdims=True), axis=1, keepdims=True)
    d_inv = dot_nt((d_act * weighted).astype(bf16), wo_ref[...]).astype(bf16).astype(f32)
    pick2 = jnp.concatenate([pick, pick], axis=1)
    scale = [2.0 * d_inv[:, i * C : (i + 1) * C] / (1.0 + sums[i]) for i in range(3)]
    which = (0, 2, 2, 2, 2, 2, 1, 1, 1)
    for part, (first, last) in enumerate(SLOPE_PARTS):
        for at in range(first, last):
            cols = slice(at * C, (at + 1) * C)
            value = mom[:, cols] * scale[which[at]]
            hi, lo = split(value)
            slope_send[:, cols] = dot(pick2, jnp.concatenate([hi, lo], axis=0))
            gt[cols, 0:A] = value.T.astype(bf16)
        if part < 2:
            for g in (1, 3, 2, 0):
                slope_copy(g, part).start()

    def stage_copy(stage, peer, slot):
        count, mine, where, buf, send, recv = stages[stage]
        return pltpu.make_async_remote_copy(
            src_ref=buf.at[mine],
            dst_ref=buf.at[slot],
            send_sem=send.at[0],
            recv_sem=recv.at[0],
            device_id=where(peer),
            device_id_type=MESH,
        )

    def stage_start(stage, value):
        count, mine, where, buf, send, recv = stages[stage]
        buf[mine] = value
        for s in range(1, count):
            stage_copy(stage, lax.rem(mine + s, count), mine).start()

    def stage_end(stage):
        count, mine, where, buf, send, recv = stages[stage]
        if count > 1:
            wait_bytes(buf.at[pl.ds(0, count - 1)], recv.at[0])
        total = buf[0]
        for i in range(1, count):
            total = total + buf[i]
        return total

    half = lax.broadcasted_iota(jnp.int32, (8, C), 0)
    pair = jnp.where(half == 0, own_energy, dom_ref[...].astype(f32))
    stage_start(0, pair)

    def pull(part, q, carry):
        first, last = SLOPE_PARTS[part]
        side = even if first < 6 else odd
        lanes = pl.ds(pl.multiple_of(q * WIDE, WIDE), WIDE)
        found = dot(gt[first * C : last * C, :], side[0:R, lanes])
        for s in range(STEP):
            k = q * STEP + s
            cols = pl.ds(pl.multiple_of(k * A, A), A)
            w, d_w = pres[:, cols], acts[:, cols]
            for at in range(first, last):
                base = (at - first) * C
                h = found[base : base + C, s * A : (s + 1) * A]
                spot = pl.ds(k * 16 + at, 1)
                if at:
                    ays[spot, :] = jnp.sum(h * w, axis=0, keepdims=True)
                bys[spot, :] = jnp.sum(h * d_w, axis=0, keepdims=True)
        return carry

    for part, (first, last) in enumerate(SLOPE_PARTS):
        wait_part(slope_recv, r3, SLOPE_PARTS, part)
        for later in ((2, 3), (4,), (5,), (), (), ())[part]:
            for g in (1, 3, 2, 0):
                slope_copy(g, later).start()
        for at in range(first, last):
            cols = slice(at * C, (at + 1) * C)
            gt[cols, A : 2 * A] = slope_recv[0:A, cols].T.astype(bf16)
            gt[cols, 2 * A : R] = slope_recv[A:NG, cols].T.astype(bf16)
        lax.fori_loop(0, K // STEP, functools.partial(pull, part), 0, unroll=4)
        if part == 2:
            stage_start(1, stage_end(0))
    stage_start(2, stage_end(1))

    g_of = {m: ays[pl.ds(at, K, stride=16), :] for at, m in enumerate(ORDER) if m}
    d_radius = bys[pl.ds(0, K, stride=16), :]
    for at in range(1, 9):
        d_radius = d_radius + bys[pl.ds(at, K, stride=16), :] * harm[at]
    inv, ux, uy, uz = geom[2], geom[3], geom[4], geom[5]
    dux = root3 * g_of[1] + root15 * (uy * g_of[4] + uz * g_of[7] + ux * g_of[8])
    duy = root3 * g_of[2] + root15 * (ux * g_of[4] + uz * g_of[5] - uy * g_of[8])
    duz = root3 * g_of[3] + root15 * (uy * g_of[5] + ux * g_of[7]) + 3.0 * root5 * uz * g_of[6]
    along = d_radius - (dux * ux + duy * uy + duz * uz) * inv
    for c, (du, u) in enumerate(((dux, ux), (duy, uy), (duz, uz))):
        value = du * inv + u * along
        hi = value.astype(bf16).astype(f32)
        brow[pl.ds(c, K, stride=NB), :] = hi
        brow[pl.ds(c + 3, K, stride=NB), :] = value - hi
    brow[pl.ds(6, K, stride=NB), :] = jnp.zeros((K, A), f32)
    brow[pl.ds(7, K, stride=NB), :] = jnp.zeros((K, A), f32)
    for k in range(K):
        ddr[:, k * A : (k + 1) * A] = brow[k * NB : (k + 1) * NB, :].astype(bf16)
    found = dot_nt(odd[0:R, :], ddr[...])
    wide_found = jnp.concatenate([found, jnp.zeros((R, A - 8), f32)], axis=1)
    full = jnp.concatenate([wide_found, jnp.zeros((3 * A - R, A), f32)], axis=0)
    flipped = [full[i * A : (i + 1) * A].T[0:8] for i in range(3)]
    fsend[0] = flipped[1]
    fsend[1] = flipped[2]

    def force_copy(g):
        return pltpu.make_async_remote_copy(
            src_ref=fsend.at[g // 2],
            dst_ref=frecv.at[g],
            send_sem=s4.at[0],
            recv_sem=r4.at[0],
            device_id=owners[g],
            device_id_type=MESH,
        )

    for g in (1, 3, 2, 0):
        force_copy(g).start()
    wait_bytes(frecv, r4.at[0])
    wide8 = lax.broadcasted_iota(jnp.int32, (8, A), 1)
    back_a = jnp.where(wide8 < GF, frecv[0], frecv[1])
    back_b = jnp.where(wide8 < GC, frecv[2], frecv[3])
    back = jnp.concatenate([back_a, back_b[:, 0 : 2 * GC]], axis=1)
    back = back + 0.0
    hi, lo = split(back)
    total = flipped[0] + dot(hi, pick) + dot(lo, pick)
    for c in range(3):
        force_out[c] = -(total[c : c + 1] + total[c + 3 : c + 4])
    sums = stage_end(2)
    energy_out[...] = sums[0:1, 0:1] / sums[1:2, 0:1]
    outs = [
        pltpu.make_async_copy(force_out, force_ref, out_sem.at[0]),
        pltpu.make_async_copy(energy_out, energy_ref, out_sem.at[1]),
    ]
    for out in outs:
        out.start()

    for out in outs:
        out.wait()
    wait_bytes(outf, s1.at[0])
    wait_bytes(outc, s1.at[1])
    wait_bytes(frecv, s4.at[0])
    for part in range(len(MOMENT_PARTS)):
        wait_part(msend, s2, MOMENT_PARTS, part)
    for part in range(len(SLOPE_PARTS)):
        wait_part(slope_send, s3, SLOPE_PARTS, part)
    for count, mine, where, buf, send, recv in stages:
        if count > 1:
            wait_bytes(buf.at[pl.ds(0, count - 1)], send.at[0])


def on_device(
    sizes,
    features,
    positions,
    neighbours,
    neighbour_counts,
    domain_counts,
    face_lists,
    corner_lists,
    w_center,
    w_neigh,
    w_radial,
    w_latent,
    w_readout,
    w_energy,
):
    nx, ny = sizes
    inner = min(nx, 8)
    outer = nx // inner
    vmem = pltpu.VMEM
    dma = pltpu.SemaphoreType.DMA
    scratch = [
        vmem((A, C), bf16),
        vmem((3, 1, A), f32),
        vmem((K, A), jnp.int32),
        vmem((1, A), jnp.int32),
        vmem((1, 1), jnp.int32),
        vmem((2, GF), jnp.int32),
        vmem((2, GC), jnp.int32),
        vmem((C, C), bf16),
        vmem((C, C), bf16),
        vmem((NB, C), f32),
        vmem((C, C), bf16),
        vmem((3 * C, C), bf16),
        vmem((1, C), f32),
        dma((13,)),
        vmem((3, 1, A), f32),
        vmem((1, 1), f32),
        dma((2,)),
        vmem((2, GF + 8, C), f32),
        vmem((2, GC + 8, C), f32),
        vmem((2, GF + 8, C), f32),
        vmem((2, GC + 8, C), f32),
        vmem((3 * A, C), f32),
        vmem((C, 3 * A), bf16),
        vmem((C, A), f32),
        vmem((R + 4 * NB, PAIRS), bf16),
        vmem((R, PAIRS), bf16),
        vmem((K * NB, A), f32),
        vmem((K * NB, A), f32),
        vmem((4 * NB, PAIRS), bf16),
        vmem((9, K, A), f32),
        vmem((9, K, 16, A), bf16),
        vmem((6, K, A), f32),
        vmem((C, PAIRS), f32),
        vmem((C, PAIRS), f32),
        vmem((9 * C, PAIRS), bf16),
        vmem((A, 9 * C), f32),
        vmem((2, R, 3 * C), f32),
        vmem((NG, 9 * C), f32),
        vmem((NG, 9 * C), f32),
        vmem((NG, 9 * C), f32),
        vmem((NG, 9 * C), f32),
        vmem((9 * C, R), bf16),
        vmem((K * 16, A), f32),
        vmem((K * 16, A), f32),
        vmem((8, PAIRS), bf16),
        vmem((2, 8, A), f32),
        vmem((4, 8, A), f32),
        vmem((inner, 8, C), f32),
        vmem((outer, 8, C), f32),
        vmem((ny, 8, C), f32),
        dma((2,)),
        dma((2,)),
        dma((len(MOMENT_PARTS),)),
        dma((len(MOMENT_PARTS),)),
        dma((len(SLOPE_PARTS),)),
        dma((len(SLOPE_PARTS),)),
        dma((1,)),
        dma((1,)),
        dma((1,)),
        dma((1,)),
        dma((1,)),
        dma((1,)),
        dma((1,)),
        dma((1,)),
    ]
    energy, forces = pl.pallas_call(
        functools.partial(kernel, sizes),
        out_shape=(
            jax.ShapeDtypeStruct((1, 1), f32),
            jax.ShapeDtypeStruct((3, 1, A), f32),
        ),
        in_specs=[pl.BlockSpec(memory_space=pltpu.HBM)] * 13,
        out_specs=(
            pl.BlockSpec(memory_space=pl.ANY),
            pl.BlockSpec(memory_space=pl.ANY),
        ),
        scratch_shapes=scratch,
        compiler_params=pltpu.CompilerParams(
            collective_id=0, has_side_effects=True, vmem_limit_bytes=61900 * 1024
        ),
    )(
        features[0, 0],
        jnp.transpose(positions, (0, 2, 1, 3))[0],
        neighbours[0, 0],
        neighbour_counts[0],
        domain_counts,
        face_lists[0, 0],
        corner_lists[0, 0],
        w_center,
        w_neigh,
        w_radial,
        w_latent,
        w_readout,
        w_energy[None, :],
    )
    return (energy.reshape(()), -jnp.transpose(forces[None], (0, 2, 1, 3)))


def solution(mesh):
    sizes = (mesh.shape["gx"], mesh.shape["gy"])
    placed = (
        P("gx", "gy", None, None),
        P("gx", "gy", None, None),
        P("gx", "gy", None, None),
        P("gx", "gy", None),
        P("gx", "gy"),
        P("gx", "gy", None, None),
        P("gx", "gy", None, None),
        P(),
        P(),
        P(),
        P(),
        P(),
        P(),
    )
    return jax.shard_map(
        functools.partial(on_device, sizes),
        mesh=mesh,
        in_specs=placed,
        out_specs=(P(), P("gx", "gy", None, None)),
        check_vma=False,
    )
```

```python
import functools
import math

import jax
import jax.numpy as jnp
from jax import lax
from jax.experimental import pallas as pl
from jax.experimental.pallas import tpu as pltpu
from jax.sharding import PartitionSpec as P

cutoff = 6.0
soften = 0.25
box_width = 4.0
f32 = jnp.float32
bf16 = jnp.bfloat16
MESH = pl.DeviceIdType.MESH

A = 128
C = 128
K = 32
GF = 64
GC = 16
NG = 2 * GF + 2 * GC
R = A + NG
NB = 8
PAIRS = K * A
STEP = 4
WIDE = STEP * A
PULL_STEP = 4
PULL_WIDE = PULL_STEP * A
ORDER = (0, 4, 5, 6, 7, 8, 1, 2, 3)
MOMENT_PARTS = ((0, 2), (2, 4), (4, 6), (6, 9))
SLOPE_PARTS = ((6, 9), (4, 6), (2, 4), (0, 2))
GROUPS = ((0, GF), (GF, GF), (2 * GF, GC), (2 * GF + GC, GC))


def dot(a, b):
    return lax.dot_general(a, b, (((1,), (0,)), ((), ())), preferred_element_type=f32)


def dot_nt(a, b):
    return lax.dot_general(a, b, (((1,), (1,)), ((), ())), preferred_element_type=f32)


def split(x):
    hi = x.astype(bf16)
    lo = (x - hi.astype(f32)).astype(bf16)
    return hi, lo


def silu_parts(x):
    s = 0.5 + 0.5 * jnp.tanh(0.5 * x)
    y = x * s
    return y, s + y * (1.0 - s)


def pick_lanes(table, index):
    return jnp.take_along_axis(table, index, axis=1)


def kernel(
    sizes,
    feat_hbm,
    pos_hbm,
    nbr_hbm,
    cnt_hbm,
    dom_hbm,
    face_hbm,
    corner_hbm,
    wc_hbm,
    wn_hbm,
    wr_hbm,
    wl_hbm,
    wo_hbm,
    we_hbm,
    energy_ref,
    force_ref,
    feat_ref,
    pos_ref,
    nbr_ref,
    cnt_ref,
    dom_ref,
    face_ref,
    corner_ref,
    wc_ref,
    wn_ref,
    wr_ref,
    wl_ref,
    wo_ref,
    we_ref,
    load_sem,
    force_out,
    energy_out,
    out_sem,
    outf,
    outc,
    inf,
    inc,
    proj,
    left,
    cent,
    even,
    odd,
    brow,
    drow,
    slow,
    harm,
    tiles,
    geom,
    pres,
    acts,
    term,
    mom,
    msend,
    mrecv,
    slope_send,
    slope_recv,
    gt,
    ays,
    bys,
    ddr,
    fsend,
    frecv,
    ebuf_a,
    ebuf_b,
    ebuf_c,
    s1,
    r1,
    s2,
    r2,
    s3,
    r3,
    s4,
    r4,
    sa,
    ra,
    sb,
    rb,
    sc,
    rc,
):
    nx, ny = sizes
    gx = lax.axis_index("gx")
    gy = lax.axis_index("gy")
    up_x, down_x = lax.rem(gx + 1, nx), lax.rem(gx + nx - 1, nx)
    up_y, down_y = lax.rem(gy + 1, ny), lax.rem(gy + ny - 1, ny)
    holders = ((down_x, gy), (gx, down_y), (down_x, down_y), (down_x, up_y))
    owners = ((up_x, gy), (gx, up_y), (up_x, up_y), (up_x, down_y))
    inner = min(nx, 8)
    outer = nx // inner
    block, place = gx // inner, lax.rem(gx, inner)

    def group_a(i):
        return (block * inner + i, gy)

    def group_b(i):
        return (i * inner + place, gy)

    def group_c(i):
        return (gx, i)

    stages = (
        (inner, place, group_a, ebuf_a, sa, ra),
        (outer, block, group_b, ebuf_b, sb, rb),
        (ny, gy, group_c, ebuf_c, sc, rc),
    )

    barrier = pltpu.get_barrier_semaphore()
    greeted = list(holders) + list(owners)
    for count, mine, where, unused_buf, unused_s, unused_r in stages:
        for s in range(1, count):
            greeted.append(where(lax.rem(mine + s, count)))
    for target in greeted:
        pl.semaphore_signal(barrier, inc=1, device_id=target, device_id_type=MESH)

    first_loads = [
        (face_hbm, face_ref),
        (corner_hbm, corner_ref),
        (feat_hbm, feat_ref),
        (pos_hbm, pos_ref),
    ]
    later_loads = [
        (nbr_hbm, nbr_ref),
        (wn_hbm, wn_ref),
        (wc_hbm, wc_ref),
        (wr_hbm, wr_ref),
        (cnt_hbm, cnt_ref),
        (dom_hbm, dom_ref),
        (wl_hbm, wl_ref),
        (wo_hbm, wo_ref),
        (we_hbm, we_ref),
    ]
    loads = [
        pltpu.make_async_copy(src, dst, load_sem.at[i])
        for i, (src, dst) in enumerate(first_loads + later_loads)
    ]
    for load in loads:
        load.start()
    for load in loads[: len(first_loads)]:
        load.wait()

    sub = lax.broadcasted_iota(jnp.int32, (A, A), 0)
    lane = lax.broadcasted_iota(jnp.int32, (A, A), 1)
    eye = jnp.where(sub == lane, 1.0, 0.0)
    lists_a = jnp.concatenate([face_ref[0:1, :], face_ref[1:2, :]], axis=1)
    none = jnp.full((1, A - 2 * GC), -1, jnp.int32)
    lists_b = jnp.concatenate([corner_ref[0:1, :], corner_ref[1:2, :], none], axis=1)
    pt_a = jnp.where(sub == lists_a, 1.0, 0.0)
    pt_b = jnp.where(sub == lists_b, 1.0, 0.0)
    pick = jnp.concatenate([pt_a.T, pt_b.T[0 : 2 * GC]], axis=0).astype(bf16)
    spread = jnp.concatenate([pt_a, pt_b], axis=1).astype(bf16)[:, 0:NG]
    feat = feat_ref[...]
    picked = dot(pick, feat)
    small = lax.broadcasted_iota(jnp.int32, (3, A), 0)
    wide = lax.broadcasted_iota(jnp.int32, (3, A), 1)
    pos = jnp.concatenate([pos_ref[c] for c in range(3)], axis=0)
    zero = jnp.zeros((3, A), f32)
    at_a = pick_lanes(pos, jnp.broadcast_to(lists_a, (3, A)))
    at_b = pick_lanes(pos, jnp.broadcast_to(jnp.maximum(lists_b, 0), (3, A)))
    at_a = at_a + jnp.where(small == jnp.where(wide < GF, 0, 1), box_width, zero)
    tilt = jnp.where(wide < GC, box_width, -box_width)
    at_b = at_b + jnp.where(small == 0, box_width, jnp.where(small == 1, tilt, zero))
    for g, (base, rows) in enumerate(GROUPS):
        buf, slot, at = (outf, g, at_a) if g < 2 else (outc, g - 2, at_b)
        buf[slot, 0:rows, :] = picked[base : base + rows]
        buf[slot, rows : rows + 8, :] = jnp.zeros((8, A), f32)
        buf[slot, rows : rows + 3, :] = at

    pl.semaphore_wait(barrier, len(greeted))

    def wait_bytes(ref, sem):
        pltpu.make_async_copy(ref, ref, sem).wait()

    def first_copy(g):
        src, dst, slot = (outf, inf, g) if g < 2 else (outc, inc, g - 2)
        return pltpu.make_async_remote_copy(
            src_ref=src.at[slot],
            dst_ref=dst.at[slot],
            send_sem=s1.at[g // 2],
            recv_sem=r1.at[g // 2],
            device_id=holders[g],
            device_id_type=MESH,
        )

    for g in (1, 3, 2, 0):
        first_copy(g).start()

    for load in loads[len(first_loads) :]:
        load.wait()

    proj[0:A, :] = dot(feat, wn_ref[...])
    center = dot(feat, wc_ref[...])
    wr = wr_ref[...]
    wr_hi = wr.astype(bf16).astype(f32)
    proj[R : R + NB, :] = wr_hi
    proj[R + NB : R + 2 * NB, :] = wr_hi
    proj[R + 2 * NB : R + 3 * NB, :] = wr - wr_hi
    proj[R + 3 * NB :, :] = jnp.zeros((384 - R - 3 * NB, C), f32)
    own_t = proj[0:A, :].T.astype(bf16)
    left[:, 0:A] = own_t
    cent[...] = center.T - own_t.astype(f32)

    sub_g = lax.broadcasted_iota(jnp.int32, (NG, A), 0) + A

    def build(k, carry):
        lanes = pl.ds(pl.multiple_of(k * A, A), A)
        index = nbr_ref[pl.ds(k, 1), :]
        own = jnp.where(sub == index, 1.0, 0.0)
        even[0:A, lanes] = (eye + own).astype(bf16)
        odd[0:A, lanes] = (eye - own).astype(bf16)
        ghost = jnp.where(sub_g == index, 1.0, 0.0)
        even[A:R, lanes] = ghost.astype(bf16)
        odd[A:R, lanes] = (-ghost).astype(bf16)
        return carry

    lax.fori_loop(0, K, build, 0)

    wait_bytes(inf, r1.at[0])
    wait_bytes(inc, r1.at[1])
    for g, (base, rows) in enumerate(GROUPS):
        buf, slot = (inf, g) if g < 2 else (inc, g - 2)
        proj[A + base : A + base + rows, :] = dot(
            buf[slot, 0:rows, :].astype(bf16), wn_ref[...]
        )
    left[:, A : 2 * A] = proj[A : 2 * A, :].T.astype(bf16)
    left[:, 2 * A : 3 * A] = proj[2 * A : 3 * A, :].T.astype(bf16)
    ghost_a = jnp.where(wide < GF, inf[0, GF : GF + 3, :], inf[1, GF : GF + 3, :])
    ghost_b = jnp.where(wide < GC, inc[0, GC : GC + 3, :], inc[1, GC : GC + 3, :])

    nbr = nbr_ref[...]
    in_own = nbr < A
    in_face = nbr < 2 * A
    local = jnp.bitwise_and(nbr, A - 1)
    delta = []
    for c in range(3):
        tables = [
            jnp.broadcast_to(t[c : c + 1, :], (K, A)) for t in (pos, ghost_a, ghost_b)
        ]
        found = [pick_lanes(t, local) for t in tables]
        other = jnp.where(in_own, found[0], jnp.where(in_face, found[1], found[2]))
        delta.append(other - tables[0])
    dx, dy, dz = delta
    radius = jnp.sqrt(dx * dx + dy * dy + dz * dz + soften)
    inv = 1.0 / radius
    ux, uy, uz = dx * inv, dy * inv, dz * inv
    t = jnp.minimum(radius / cutoff, 1.0)
    t2 = t * t
    t5 = t2 * t2 * t
    t6 = t5 * t
    envelope = 1.0 + t6 * (-28.0 + t * (48.0 - 21.0 * t))
    slot_no = lax.broadcasted_iota(jnp.int32, (K, A), 0)
    atom_no = lax.broadcasted_iota(jnp.int32, (K, A), 1)
    alive = jnp.logical_and(slot_no < cnt_ref[...], atom_no < dom_ref[...])
    live = jnp.where(alive, 1.0, 0.0)
    root3, root5, root15 = math.sqrt(3.0), math.sqrt(5.0), math.sqrt(15.0)
    y_all = (
        None,
        root3 * ux,
        root3 * uy,
        root3 * uz,
        root15 * ux * uy,
        root15 * uy * uz,
        0.5 * root5 * (3.0 * uz * uz - 1.0),
        root15 * ux * uz,
        0.5 * root15 * (ux * ux - uy * uy),
    )
    for q, m in enumerate(ORDER):
        if m:
            harm[q] = y_all[m]
    geom[0] = envelope * live
    geom[1] = live * (t5 * (-168.0 + t * (336.0 - 168.0 * t)) * jnp.where(radius < cutoff, 1.0 / cutoff, 0.0))
    geom[2], geom[3], geom[4], geom[5] = inv, ux, uy, uz
    theta = radius * (math.pi / cutoff)
    sin1, cos1 = jnp.sin(theta), jnp.cos(theta)
    norm = math.sqrt(2.0 / cutoff)
    s_old, s_now = jnp.zeros_like(theta), sin1
    c_old, c_now = jnp.ones_like(theta), cos1
    for n in range(1, NB + 1):
        value = norm * s_now * inv
        brow[pl.ds(n - 1, K, stride=NB), :] = value
        drow[pl.ds(n - 1, K, stride=NB), :] = (
            norm * (n * math.pi / cutoff) * c_now * inv - value * inv
        )
        s_old, s_now = s_now, 2.0 * cos1 * s_now - s_old
        c_old, c_now = c_now, 2.0 * cos1 * c_now - c_old

    def put_basis(k, carry):
        lanes = pl.ds(pl.multiple_of(k * A, A), A)
        tile = brow[pl.ds(pl.multiple_of(k * NB, NB), NB), :]
        hi = tile.astype(bf16).astype(f32)
        rows = jnp.concatenate([hi, tile - hi, hi, jnp.zeros_like(hi)], axis=0)
        even[R : R + 4 * NB, lanes] = rows.astype(bf16)
        tile = drow[pl.ds(pl.multiple_of(k * NB, NB), NB), :]
        hi = tile.astype(bf16).astype(f32)
        rows = jnp.concatenate([hi, tile - hi, hi, jnp.zeros_like(hi)], axis=0)
        slow[:, lanes] = rows.astype(bf16)
        for at in range(1, 9):
            row = jnp.broadcast_to(harm[at, pl.ds(k, 1), :], (16, A))
            tiles[at, pl.ds(k, 1)] = row.astype(bf16)[None]
        return carry

    lax.fori_loop(0, K, put_basis, 0)

    wl_t = wl_ref[...].astype(f32).T.astype(bf16)
    cent_wide = jnp.concatenate([cent[...]] * STEP, axis=1)

    def forward(q, carry):
        lanes = pl.ds(pl.multiple_of(q * WIDE, WIDE), WIDE)
        pre = dot(left[:, 0 : R + 4 * NB], even[:, lanes]) + cent_wide
        pres[:, lanes] = pre
        hidden = pre * (0.5 + 0.5 * jnp.tanh(0.5 * pre))
        act = dot(wl_t, hidden.astype(bf16))
        acts[:, lanes] = act
        latent = act * (0.5 + 0.5 * jnp.tanh(0.5 * act))
        for s in range(STEP):
            k = q * STEP + s
            cols = pl.ds(pl.multiple_of(k * A, A), A)
            w = latent[:, s * A : (s + 1) * A] * geom[0, pl.ds(k, 1), :]
            term[0:C, cols] = w.astype(bf16)
        return carry

    lax.fori_loop(0, K // STEP, forward, 0, unroll=8)

    def group_copy(src, dst, send, recv, g, part, targets, parts):
        base, rows = GROUPS[g]
        first, last = parts[part]
        view = (pl.ds(base, rows), pl.ds(first * C, (last - first) * C))
        return pltpu.make_async_remote_copy(
            src_ref=src.at[view],
            dst_ref=dst.at[view],
            send_sem=send.at[part],
            recv_sem=recv.at[part],
            device_id=targets[g],
            device_id_type=MESH,
        )

    def wait_part(ref, sem, parts, part):
        first, last = parts[part]
        wait_bytes(ref.at[:, pl.ds(first * C, (last - first) * C)], sem.at[part])

    def moment_copy(g, part):
        return group_copy(msend, mrecv, s2, r2, g, part, owners, MOMENT_PARTS)

    def slope_copy(g, part):
        return group_copy(slope_send, slope_recv, s3, r3, g, part, holders, SLOPE_PARTS)

    def build_terms(first, last):
        for at in range(max(first, 1), last):
            for k in range(K):
                cols = slice(k * A, (k + 1) * A)
                tile = jnp.concatenate([tiles[at, k]] * (C // 16), axis=0)
                term[at * C : (at + 1) * C, cols] = term[0:C, cols] * tile

    build_terms(*MOMENT_PARTS[0])
    for part, (first, last) in enumerate(MOMENT_PARTS):
        if part + 1 < len(MOMENT_PARTS):
            build_terms(*MOMENT_PARTS[part + 1])
        cols = slice(first * C, last * C)
        side = even if first < 6 else odd
        size = (last - first) * C
        found = dot_nt(side[0:R, :], term[cols, :])
        mom[:, cols] = found[0:A]
        msend[:, cols] = found[A:R]
        for g in (1, 3, 2, 0):
            moment_copy(g, part).start()

    def slope_of_latents(q, carry):
        lanes = pl.ds(pl.multiple_of(q * WIDE, WIDE), WIDE)
        unused_hidden, d1 = silu_parts(pres[:, lanes])
        d_hidden = d1 * dot(left[:, R : R + 4 * NB], slow[:, lanes])
        latent, d2 = silu_parts(acts[:, lanes])
        d_latent = d2 * dot(wl_t, d_hidden.astype(bf16))
        for s in range(STEP):
            k = q * STEP + s
            cols = pl.ds(pl.multiple_of(k * A, A), A)
            here = slice(s * A, (s + 1) * A)
            env, d_env = geom[0, pl.ds(k, 1), :], geom[1, pl.ds(k, 1), :]
            pres[:, cols] = latent[:, here] * env
            acts[:, cols] = d_latent[:, here] * env + latent[:, here] * d_env
        return carry

    lax.fori_loop(0, K // STEP, slope_of_latents, 0, unroll=4)

    spread2 = jnp.concatenate([spread, spread], axis=1)
    for part, (first, last) in enumerate(MOMENT_PARTS):
        cols = slice(first * C, last * C)
        wait_part(mrecv, r2, MOMENT_PARTS, part)
        hi, lo = split(mrecv[:, cols])
        mom[:, cols] = mom[:, cols] + dot(spread2, jnp.concatenate([hi, lo], axis=0))

    levels = ((0, 1), (6, 9), (1, 6))
    sums = []
    for first, last in levels:
        total = None
        for at in range(first, last):
            value = mom[:, at * C : (at + 1) * C]
            total = value * value if total is None else total + value * value
        sums.append(total)
    packed = jnp.concatenate([jnp.log1p(x) for x in sums], axis=1).astype(bf16)
    inner_act = dot(packed, wo_ref[...])
    act, d_act = silu_parts(inner_act)
    row_live = jnp.where(sub < dom_ref[...], 1.0, 0.0)
    weighted = row_live * we_ref[...]
    own_energy = jnp.sum(jnp.sum(act * weighted, axis=0, keepdims=True), axis=1, keepdims=True)
    d_inv = dot_nt((d_act * weighted).astype(bf16), wo_ref[...]).astype(bf16).astype(f32)
    pick2 = jnp.concatenate([pick, pick], axis=1)
    scale = [2.0 * d_inv[:, i * C : (i + 1) * C] / (1.0 + sums[i]) for i in range(3)]
    which = (0, 2, 2, 2, 2, 2, 1, 1, 1)
    for part, (first, last) in enumerate(SLOPE_PARTS):
        for at in range(first, last):
            cols = slice(at * C, (at + 1) * C)
            value = mom[:, cols] * scale[which[at]]
            hi, lo = split(value)
            slope_send[:, cols] = dot(pick2, jnp.concatenate([hi, lo], axis=0))
            gt[cols, 0:A] = value.T.astype(bf16)
        if part < 2:
            for g in (1, 3, 2, 0):
                slope_copy(g, part).start()

    def stage_copy(stage, peer, slot):
        count, mine, where, buf, send, recv = stages[stage]
        return pltpu.make_async_remote_copy(
            src_ref=buf.at[mine],
            dst_ref=buf.at[slot],
            send_sem=send.at[0],
            recv_sem=recv.at[0],
            device_id=where(peer),
            device_id_type=MESH,
        )

    def stage_start(stage, value):
        count, mine, where, buf, send, recv = stages[stage]
        buf[mine] = value
        for s in range(1, count):
            stage_copy(stage, lax.rem(mine + s, count), mine).start()

    def stage_end(stage):
        count, mine, where, buf, send, recv = stages[stage]
        if count > 1:
            wait_bytes(buf.at[pl.ds(0, count - 1)], recv.at[0])
        total = buf[0]
        for i in range(1, count):
            total = total + buf[i]
        return total

    half = lax.broadcasted_iota(jnp.int32, (8, C), 0)
    pair = jnp.where(half == 0, own_energy, dom_ref[...].astype(f32))
    stage_start(0, pair)

    def pull(part, q, carry):
        first, last = SLOPE_PARTS[part]
        side = even if first < 6 else odd
        lanes = pl.ds(pl.multiple_of(q * PULL_WIDE, PULL_WIDE), PULL_WIDE)
        found = dot(gt[first * C : last * C, :], side[0:R, lanes])
        for s in range(PULL_STEP):
            k = q * PULL_STEP + s
            cols = pl.ds(pl.multiple_of(k * A, A), A)
            w, d_w = pres[:, cols], acts[:, cols]
            for at in range(first, last):
                base = (at - first) * C
                h = found[base : base + C, s * A : (s + 1) * A]
                spot = pl.ds(k * 16 + at, 1)
                if at:
                    ays[spot, :] = jnp.sum(h * w, axis=0, keepdims=True)
                bys[spot, :] = jnp.sum(h * d_w, axis=0, keepdims=True)
        return carry

    def pull_all(part):
        step = functools.partial(pull, part)
        lax.fori_loop(0, K // PULL_STEP, step, 0, unroll=8)

    for part, (first, last) in enumerate(SLOPE_PARTS):
        wait_part(slope_recv, r3, SLOPE_PARTS, part)
        for later in ((2,), (3,), (), ())[part]:
            for g in (1, 3, 2, 0):
                slope_copy(g, later).start()
        for at in range(first, last):
            cols = slice(at * C, (at + 1) * C)
            gt[cols, A : 2 * A] = slope_recv[0:A, cols].T.astype(bf16)
            gt[cols, 2 * A : R] = slope_recv[A:NG, cols].T.astype(bf16)
        pull_all(part)
        if part == 1:
            stage_start(1, stage_end(0))
    stage_start(2, stage_end(1))

    g_of = {m: ays[pl.ds(at, K, stride=16), :] for at, m in enumerate(ORDER) if m}
    d_radius = bys[pl.ds(0, K, stride=16), :]
    for at in range(1, 9):
        d_radius = d_radius + bys[pl.ds(at, K, stride=16), :] * harm[at]
    inv, ux, uy, uz = geom[2], geom[3], geom[4], geom[5]
    dux = root3 * g_of[1] + root15 * (uy * g_of[4] + uz * g_of[7] + ux * g_of[8])
    duy = root3 * g_of[2] + root15 * (ux * g_of[4] + uz * g_of[5] - uy * g_of[8])
    duz = root3 * g_of[3] + root15 * (uy * g_of[5] + ux * g_of[7]) + 3.0 * root5 * uz * g_of[6]
    along = d_radius - (dux * ux + duy * uy + duz * uz) * inv
    for c, (du, u) in enumerate(((dux, ux), (duy, uy), (duz, uz))):
        value = du * inv + u * along
        hi = value.astype(bf16).astype(f32)
        brow[pl.ds(c, K, stride=NB), :] = hi
        brow[pl.ds(c + 3, K, stride=NB), :] = value - hi
    brow[pl.ds(6, K, stride=NB), :] = jnp.zeros((K, A), f32)
    brow[pl.ds(7, K, stride=NB), :] = jnp.zeros((K, A), f32)
    for k in range(K):
        ddr[:, k * A : (k + 1) * A] = brow[k * NB : (k + 1) * NB, :].astype(bf16)
    found = dot_nt(odd[0:R, :], ddr[...])
    wide_found = jnp.concatenate([found, jnp.zeros((R, A - 8), f32)], axis=1)
    full = jnp.concatenate([wide_found, jnp.zeros((3 * A - R, A), f32)], axis=0)
    flipped = [full[i * A : (i + 1) * A].T[0:8] for i in range(3)]
    fsend[0] = flipped[1]
    fsend[1] = flipped[2]

    def force_copy(g):
        return pltpu.make_async_remote_copy(
            src_ref=fsend.at[g // 2],
            dst_ref=frecv.at[g],
            send_sem=s4.at[0],
            recv_sem=r4.at[0],
            device_id=owners[g],
            device_id_type=MESH,
        )

    for g in (1, 3, 2, 0):
        force_copy(g).start()
    wait_bytes(frecv, r4.at[0])
    wide8 = lax.broadcasted_iota(jnp.int32, (8, A), 1)
    back_a = jnp.where(wide8 < GF, frecv[0], frecv[1])
    back_b = jnp.where(wide8 < GC, frecv[2], frecv[3])
    back = jnp.concatenate([back_a, back_b[:, 0 : 2 * GC]], axis=1)
    back = back + 0.0
    hi, lo = split(back)
    total = flipped[0] + dot(hi, pick) + dot(lo, pick)
    for c in range(3):
        force_out[c] = -(total[c : c + 1] + total[c + 3 : c + 4])
    sums = stage_end(2)
    energy_out[...] = sums[0:1, 0:1] / sums[1:2, 0:1]
    outs = [
        pltpu.make_async_copy(force_out, force_ref, out_sem.at[0]),
        pltpu.make_async_copy(energy_out, energy_ref, out_sem.at[1]),
    ]
    for out in outs:
        out.start()

    for out in outs:
        out.wait()
    wait_bytes(outf, s1.at[0])
    wait_bytes(outc, s1.at[1])
    wait_bytes(frecv, s4.at[0])
    for part in range(len(MOMENT_PARTS)):
        wait_part(msend, s2, MOMENT_PARTS, part)
    for part in range(len(SLOPE_PARTS)):
        wait_part(slope_send, s3, SLOPE_PARTS, part)
    for count, mine, where, buf, send, recv in stages:
        if count > 1:
            wait_bytes(buf.at[pl.ds(0, count - 1)], send.at[0])


def on_device(
    sizes,
    features,
    positions,
    neighbours,
    neighbour_counts,
    domain_counts,
    face_lists,
    corner_lists,
    w_center,
    w_neigh,
    w_radial,
    w_latent,
    w_readout,
    w_energy,
):
    nx, ny = sizes
    inner = min(nx, 8)
    outer = nx // inner
    vmem = pltpu.VMEM
    dma = pltpu.SemaphoreType.DMA
    scratch = [
        vmem((A, C), bf16),
        vmem((3, 1, A), f32),
        vmem((K, A), jnp.int32),
        vmem((1, A), jnp.int32),
        vmem((1, 1), jnp.int32),
        vmem((2, GF), jnp.int32),
        vmem((2, GC), jnp.int32),
        vmem((C, C), bf16),
        vmem((C, C), bf16),
        vmem((NB, C), f32),
        vmem((C, C), bf16),
        vmem((3 * C, C), bf16),
        vmem((1, C), f32),
        dma((13,)),
        vmem((3, 1, A), f32),
        vmem((1, 1), f32),
        dma((2,)),
        vmem((2, GF + 8, C), f32),
        vmem((2, GC + 8, C), f32),
        vmem((2, GF + 8, C), f32),
        vmem((2, GC + 8, C), f32),
        vmem((3 * A, C), f32),
        vmem((C, 3 * A), bf16),
        vmem((C, A), f32),
        vmem((R + 4 * NB, PAIRS), bf16),
        vmem((R, PAIRS), bf16),
        vmem((K * NB, A), f32),
        vmem((K * NB, A), f32),
        vmem((4 * NB, PAIRS), bf16),
        vmem((9, K, A), f32),
        vmem((9, K, 16, A), bf16),
        vmem((6, K, A), f32),
        vmem((C, PAIRS), f32),
        vmem((C, PAIRS), f32),
        vmem((9 * C, PAIRS), bf16),
        vmem((A, 9 * C), f32),
        vmem((NG, 9 * C), f32),
        vmem((NG, 9 * C), f32),
        vmem((NG, 9 * C), f32),
        vmem((NG, 9 * C), f32),
        vmem((9 * C, R), bf16),
        vmem((K * 16, A), f32),
        vmem((K * 16, A), f32),
        vmem((8, PAIRS), bf16),
        vmem((2, 8, A), f32),
        vmem((4, 8, A), f32),
        vmem((inner, 8, C), f32),
        vmem((outer, 8, C), f32),
        vmem((ny, 8, C), f32),
        dma((2,)),
        dma((2,)),
        dma((len(MOMENT_PARTS),)),
        dma((len(MOMENT_PARTS),)),
        dma((len(SLOPE_PARTS),)),
        dma((len(SLOPE_PARTS),)),
        dma((1,)),
        dma((1,)),
        dma((1,)),
        dma((1,)),
        dma((1,)),
        dma((1,)),
        dma((1,)),
        dma((1,)),
    ]
    energy, forces = pl.pallas_call(
        functools.partial(kernel, sizes),
        out_shape=(
            jax.ShapeDtypeStruct((1, 1), f32),
            jax.ShapeDtypeStruct((3, 1, A), f32),
        ),
        in_specs=[pl.BlockSpec(memory_space=pltpu.HBM)] * 13,
        out_specs=(
            pl.BlockSpec(memory_space=pl.ANY),
            pl.BlockSpec(memory_space=pl.ANY),
        ),
        scratch_shapes=scratch,
        compiler_params=pltpu.CompilerParams(
            collective_id=0, has_side_effects=True, vmem_limit_bytes=61900 * 1024
        ),
    )(
        features[0, 0],
        jnp.transpose(positions, (0, 2, 1, 3))[0],
        neighbours[0, 0],
        neighbour_counts[0],
        domain_counts,
        face_lists[0, 0],
        corner_lists[0, 0],
        w_center,
        w_neigh,
        w_radial,
        w_latent,
        w_readout,
        w_energy[None, :],
    )
    return (energy.reshape(()), -jnp.transpose(forces[None], (0, 2, 1, 3)))


def solution(mesh):
    sizes = (mesh.shape["gx"], mesh.shape["gy"])
    placed = (
        P("gx", "gy", None, None),
        P("gx", "gy", None, None),
        P("gx", "gy", None, None),
        P("gx", "gy", None),
        P("gx", "gy"),
        P("gx", "gy", None, None),
        P("gx", "gy", None, None),
        P(),
        P(),
        P(),
        P(),
        P(),
        P(),
    )
    return jax.shard_map(
        functools.partial(on_device, sizes),
        mesh=mesh,
        in_specs=placed,
        out_specs=(P(), P("gx", "gy", None, None)),
        check_vma=False,
    )
```

```python
import functools
import math

import jax
import jax.numpy as jnp
from jax import lax
from jax.experimental import pallas as pl
from jax.experimental.pallas import tpu as pltpu
from jax.sharding import PartitionSpec as P

cutoff = 6.0
soften = 0.25
box_width = 4.0
f32 = jnp.float32
bf16 = jnp.bfloat16
MESH = pl.DeviceIdType.MESH

A = 128
C = 128
K = 32
GF = 64
GC = 16
NG = 2 * GF + 2 * GC
R = A + NG
NB = 8
PAIRS = K * A
STEP = 4
WIDE = STEP * A
PULL_STEP = 4
PULL_WIDE = PULL_STEP * A
ORDER = (0, 4, 5, 6, 7, 8, 1, 2, 3)
MOMENT_PARTS = ((0, 2), (2, 4), (4, 6), (6, 9))
SLOPE_PARTS = ((6, 9), (4, 6), (2, 4), (0, 2))
GROUPS = ((0, GF), (GF, GF), (2 * GF, GC), (2 * GF + GC, GC))


def dot(a, b):
    return lax.dot_general(a, b, (((1,), (0,)), ((), ())), preferred_element_type=f32)


def dot_nt(a, b):
    return lax.dot_general(a, b, (((1,), (1,)), ((), ())), preferred_element_type=f32)


def split(x):
    hi = x.astype(bf16)
    lo = (x - hi.astype(f32)).astype(bf16)
    return hi, lo


def silu_parts(x):
    s = 0.5 + 0.5 * jnp.tanh(0.5 * x)
    y = x * s
    return y, s + y * (1.0 - s)


def pick_lanes(table, index):
    return jnp.take_along_axis(table, index, axis=1)


def kernel(
    sizes,
    feat_hbm,
    pos_hbm,
    nbr_hbm,
    cnt_hbm,
    dom_hbm,
    face_hbm,
    corner_hbm,
    wc_hbm,
    wn_hbm,
    wr_hbm,
    wl_hbm,
    wo_hbm,
    we_hbm,
    energy_ref,
    force_ref,
    feat_ref,
    pos_ref,
    nbr_ref,
    cnt_ref,
    dom_ref,
    face_ref,
    corner_ref,
    wc_ref,
    wn_ref,
    wr_ref,
    wl_ref,
    wo_ref,
    we_ref,
    load_sem,
    force_out,
    energy_out,
    out_sem,
    outf,
    outc,
    inf,
    inc,
    proj,
    left,
    cent,
    even,
    odd,
    brow,
    drow,
    slow,
    harm,
    tiles,
    geom,
    pres,
    acts,
    term,
    mom,
    msend,
    mrecv,
    slope_send,
    slope_recv,
    gt,
    ays,
    bys,
    ddr,
    fsend,
    frecv,
    ebuf_a,
    ebuf_b,
    ebuf_c,
    s1,
    r1,
    s2,
    r2,
    s3,
    r3,
    s4,
    r4,
    sa,
    ra,
    sb,
    rb,
    sc,
    rc,
):
    nx, ny = sizes
    gx = lax.axis_index("gx")
    gy = lax.axis_index("gy")
    up_x, down_x = lax.rem(gx + 1, nx), lax.rem(gx + nx - 1, nx)
    up_y, down_y = lax.rem(gy + 1, ny), lax.rem(gy + ny - 1, ny)
    holders = ((down_x, gy), (gx, down_y), (down_x, down_y), (down_x, up_y))
    owners = ((up_x, gy), (gx, up_y), (up_x, up_y), (up_x, down_y))
    inner = min(nx, 8)
    outer = nx // inner
    block, place = gx // inner, lax.rem(gx, inner)

    def group_a(i):
        return (block * inner + i, gy)

    def group_b(i):
        return (i * inner + place, gy)

    def group_c(i):
        return (gx, i)

    stages = (
        (inner, place, group_a, ebuf_a, sa, ra),
        (outer, block, group_b, ebuf_b, sb, rb),
        (ny, gy, group_c, ebuf_c, sc, rc),
    )

    barrier = pltpu.get_barrier_semaphore()
    greeted = list(holders) + list(owners)
    for count, mine, where, unused_buf, unused_s, unused_r in stages:
        for s in range(1, count):
            greeted.append(where(lax.rem(mine + s, count)))
    for target in greeted:
        pl.semaphore_signal(barrier, inc=1, device_id=target, device_id_type=MESH)

    first_loads = [
        (face_hbm, face_ref),
        (corner_hbm, corner_ref),
        (feat_hbm, feat_ref),
        (pos_hbm, pos_ref),
    ]
    later_loads = [
        (nbr_hbm, nbr_ref),
        (wn_hbm, wn_ref),
        (wc_hbm, wc_ref),
        (wr_hbm, wr_ref),
        (cnt_hbm, cnt_ref),
        (dom_hbm, dom_ref),
        (wl_hbm, wl_ref),
        (wo_hbm, wo_ref),
        (we_hbm, we_ref),
    ]
    loads = [
        pltpu.make_async_copy(src, dst, load_sem.at[i])
        for i, (src, dst) in enumerate(first_loads + later_loads)
    ]
    for load in loads:
        load.start()
    for load in loads[: len(first_loads)]:
        load.wait()

    sub = lax.broadcasted_iota(jnp.int32, (A, A), 0)
    lane = lax.broadcasted_iota(jnp.int32, (A, A), 1)
    eye = jnp.where(sub == lane, 1.0, 0.0)
    lists_a = jnp.concatenate([face_ref[0:1, :], face_ref[1:2, :]], axis=1)
    none = jnp.full((1, A - 2 * GC), -1, jnp.int32)
    lists_b = jnp.concatenate([corner_ref[0:1, :], corner_ref[1:2, :], none], axis=1)
    pt_a = jnp.where(sub == lists_a, 1.0, 0.0)
    pt_b = jnp.where(sub == lists_b, 1.0, 0.0)
    pick = jnp.concatenate([pt_a.T, pt_b.T[0 : 2 * GC]], axis=0).astype(bf16)
    spread = jnp.concatenate([pt_a, pt_b], axis=1).astype(bf16)[:, 0:NG]
    feat = feat_ref[...]
    picked = dot(pick, feat)
    small = lax.broadcasted_iota(jnp.int32, (3, A), 0)
    wide = lax.broadcasted_iota(jnp.int32, (3, A), 1)
    pos = jnp.concatenate([pos_ref[c] for c in range(3)], axis=0)
    zero = jnp.zeros((3, A), f32)
    at_a = pick_lanes(pos, jnp.broadcast_to(lists_a, (3, A)))
    at_b = pick_lanes(pos, jnp.broadcast_to(jnp.maximum(lists_b, 0), (3, A)))
    at_a = at_a + jnp.where(small == jnp.where(wide < GF, 0, 1), box_width, zero)
    tilt = jnp.where(wide < GC, box_width, -box_width)
    at_b = at_b + jnp.where(small == 0, box_width, jnp.where(small == 1, tilt, zero))
    for g, (base, rows) in enumerate(GROUPS):
        buf, slot, at = (outf, g, at_a) if g < 2 else (outc, g - 2, at_b)
        buf[slot, 0:rows, :] = picked[base : base + rows]
        buf[slot, rows : rows + 8, :] = jnp.zeros((8, A), f32)
        buf[slot, rows : rows + 3, :] = at

    pl.semaphore_wait(barrier, len(greeted))

    def wait_bytes(ref, sem):
        pltpu.make_async_copy(ref, ref, sem).wait()

    def first_copy(g):
        src, dst, slot = (outf, inf, g) if g < 2 else (outc, inc, g - 2)
        return pltpu.make_async_remote_copy(
            src_ref=src.at[slot],
            dst_ref=dst.at[slot],
            send_sem=s1.at[g // 2],
            recv_sem=r1.at[g // 2],
            device_id=holders[g],
            device_id_type=MESH,
        )

    for g in (1, 3, 2, 0):
        first_copy(g).start()

    for load in loads[len(first_loads) :]:
        load.wait()

    proj[0:A, :] = dot(feat, wn_ref[...])
    center = dot(feat, wc_ref[...])
    wr = wr_ref[...]
    wr_hi = wr.astype(bf16).astype(f32)
    proj[R : R + NB, :] = wr_hi
    proj[R + NB : R + 2 * NB, :] = wr_hi
    proj[R + 2 * NB : R + 3 * NB, :] = wr - wr_hi
    proj[R + 3 * NB :, :] = jnp.zeros((384 - R - 3 * NB, C), f32)
    own_t = proj[0:A, :].T.astype(bf16)
    left[:, 0:A] = own_t
    cent[...] = center.T - own_t.astype(f32)

    sub_g = lax.broadcasted_iota(jnp.int32, (NG, A), 0) + A

    def build(k, carry):
        lanes = pl.ds(pl.multiple_of(k * A, A), A)
        index = nbr_ref[pl.ds(k, 1), :]
        own = jnp.where(sub == index, 1.0, 0.0)
        even[0:A, lanes] = (eye + own).astype(bf16)
        odd[0:A, lanes] = (eye - own).astype(bf16)
        ghost = jnp.where(sub_g == index, 1.0, 0.0)
        even[A:R, lanes] = ghost.astype(bf16)
        odd[A:R, lanes] = (-ghost).astype(bf16)
        return carry

    lax.fori_loop(0, K, build, 0)

    wait_bytes(inf, r1.at[0])
    wait_bytes(inc, r1.at[1])
    for g, (base, rows) in enumerate(GROUPS):
        buf, slot = (inf, g) if g < 2 else (inc, g - 2)
        proj[A + base : A + base + rows, :] = dot(
            buf[slot, 0:rows, :].astype(bf16), wn_ref[...]
        )
    left[:, A : 2 * A] = proj[A : 2 * A, :].T.astype(bf16)
    left[:, 2 * A : 3 * A] = proj[2 * A : 3 * A, :].T.astype(bf16)
    ghost_a = jnp.where(wide < GF, inf[0, GF : GF + 3, :], inf[1, GF : GF + 3, :])
    ghost_b = jnp.where(wide < GC, inc[0, GC : GC + 3, :], inc[1, GC : GC + 3, :])

    nbr = nbr_ref[...]
    in_own = nbr < A
    in_face = nbr < 2 * A
    local = jnp.bitwise_and(nbr, A - 1)
    delta = []
    for c in range(3):
        tables = [
            jnp.broadcast_to(t[c : c + 1, :], (K, A)) for t in (pos, ghost_a, ghost_b)
        ]
        found = [pick_lanes(t, local) for t in tables]
        other = jnp.where(in_own, found[0], jnp.where(in_face, found[1], found[2]))
        delta.append(other - tables[0])
    dx, dy, dz = delta
    radius = jnp.sqrt(dx * dx + dy * dy + dz * dz + soften)
    inv = 1.0 / radius
    ux, uy, uz = dx * inv, dy * inv, dz * inv
    t = jnp.minimum(radius / cutoff, 1.0)
    t2 = t * t
    t5 = t2 * t2 * t
    t6 = t5 * t
    envelope = 1.0 + t6 * (-28.0 + t * (48.0 - 21.0 * t))
    slot_no = lax.broadcasted_iota(jnp.int32, (K, A), 0)
    atom_no = lax.broadcasted_iota(jnp.int32, (K, A), 1)
    alive = jnp.logical_and(slot_no < cnt_ref[...], atom_no < dom_ref[...])
    live = jnp.where(alive, 1.0, 0.0)
    root3, root5, root15 = math.sqrt(3.0), math.sqrt(5.0), math.sqrt(15.0)
    y_all = (
        None,
        root3 * ux,
        root3 * uy,
        root3 * uz,
        root15 * ux * uy,
        root15 * uy * uz,
        0.5 * root5 * (3.0 * uz * uz - 1.0),
        root15 * ux * uz,
        0.5 * root15 * (ux * ux - uy * uy),
    )
    for q, m in enumerate(ORDER):
        if m:
            harm[q] = y_all[m]
    geom[0] = envelope * live
    geom[1] = live * (t5 * (-168.0 + t * (336.0 - 168.0 * t)) * jnp.where(radius < cutoff, 1.0 / cutoff, 0.0))
    geom[2], geom[3], geom[4], geom[5] = inv, ux, uy, uz
    theta = radius * (math.pi / cutoff)
    sin1, cos1 = jnp.sin(theta), jnp.cos(theta)
    norm = math.sqrt(2.0 / cutoff)
    s_old, s_now = jnp.zeros_like(theta), sin1
    c_old, c_now = jnp.ones_like(theta), cos1
    for n in range(1, NB + 1):
        value = norm * s_now * inv
        brow[pl.ds(n - 1, K, stride=NB), :] = value
        drow[pl.ds(n - 1, K, stride=NB), :] = (
            norm * (n * math.pi / cutoff) * c_now * inv - value * inv
        )
        s_old, s_now = s_now, 2.0 * cos1 * s_now - s_old
        c_old, c_now = c_now, 2.0 * cos1 * c_now - c_old

    def put_basis(k, carry):
        lanes = pl.ds(pl.multiple_of(k * A, A), A)
        tile = brow[pl.ds(pl.multiple_of(k * NB, NB), NB), :]
        hi = tile.astype(bf16).astype(f32)
        rows = jnp.concatenate([hi, tile - hi, hi, jnp.zeros_like(hi)], axis=0)
        even[R : R + 4 * NB, lanes] = rows.astype(bf16)
        tile = drow[pl.ds(pl.multiple_of(k * NB, NB), NB), :]
        hi = tile.astype(bf16).astype(f32)
        rows = jnp.concatenate([hi, tile - hi, hi, jnp.zeros_like(hi)], axis=0)
        slow[:, lanes] = rows.astype(bf16)
        for at in range(1, 9):
            row = jnp.broadcast_to(harm[at, pl.ds(k, 1), :], (16, A))
            tiles[at, pl.ds(k, 1)] = row.astype(bf16)[None]
        return carry

    lax.fori_loop(0, K, put_basis, 0)

    wl_t = wl_ref[...].astype(f32).T.astype(bf16)
    cent_wide = jnp.concatenate([cent[...]] * STEP, axis=1)

    def forward(q, carry):
        lanes = pl.ds(pl.multiple_of(q * WIDE, WIDE), WIDE)
        pre = dot(left[:, 0 : R + 4 * NB], even[:, lanes]) + cent_wide
        pres[:, lanes] = pre
        hidden = pre * (0.5 + 0.5 * jnp.tanh(0.5 * pre))
        act = dot(wl_t, hidden.astype(bf16))
        acts[:, lanes] = act
        latent = act * (0.5 + 0.5 * jnp.tanh(0.5 * act))
        for s in range(STEP):
            k = q * STEP + s
            cols = pl.ds(pl.multiple_of(k * A, A), A)
            w = latent[:, s * A : (s + 1) * A] * geom[0, pl.ds(k, 1), :]
            term[0:C, cols] = w.astype(bf16)
        return carry

    lax.fori_loop(0, K // STEP, forward, 0, unroll=8)

    def group_copy(src, dst, send, recv, g, part, targets):
        base, rows = GROUPS[g]
        view = pl.ds(base, rows)
        return pltpu.make_async_remote_copy(
            src_ref=src[part].at[view],
            dst_ref=dst[part].at[view],
            send_sem=send.at[part],
            recv_sem=recv.at[part],
            device_id=targets[g],
            device_id_type=MESH,
        )

    def wait_part(refs, sem, part):
        wait_bytes(refs[part], sem.at[part])

    def moment_copy(g, part):
        return group_copy(msend, mrecv, s2, r2, g, part, owners)

    def slope_copy(g, part):
        return group_copy(slope_send, slope_recv, s3, r3, g, part, holders)

    def build_terms(first, last):
        for at in range(max(first, 1), last):
            for k in range(K):
                cols = slice(k * A, (k + 1) * A)
                tile = jnp.concatenate([tiles[at, k]] * (C // 16), axis=0)
                term[at * C : (at + 1) * C, cols] = term[0:C, cols] * tile

    build_terms(*MOMENT_PARTS[0])
    for part, (first, last) in enumerate(MOMENT_PARTS):
        if part + 1 < len(MOMENT_PARTS):
            build_terms(*MOMENT_PARTS[part + 1])
        cols = slice(first * C, last * C)
        side = even if first < 6 else odd
        size = (last - first) * C
        found = dot_nt(side[0:R, :], term[cols, :])
        mom[:, cols] = found[0:A]
        msend[part][...] = found[A:R]
        for g in (1, 3, 2, 0):
            moment_copy(g, part).start()

    def slope_of_latents(q, carry):
        lanes = pl.ds(pl.multiple_of(q * WIDE, WIDE), WIDE)
        unused_hidden, d1 = silu_parts(pres[:, lanes])
        d_hidden = d1 * dot(left[:, R : R + 4 * NB], slow[:, lanes])
        latent, d2 = silu_parts(acts[:, lanes])
        d_latent = d2 * dot(wl_t, d_hidden.astype(bf16))
        for s in range(STEP):
            k = q * STEP + s
            cols = pl.ds(pl.multiple_of(k * A, A), A)
            here = slice(s * A, (s + 1) * A)
            env, d_env = geom[0, pl.ds(k, 1), :], geom[1, pl.ds(k, 1), :]
            pres[:, cols] = latent[:, here] * env
            acts[:, cols] = d_latent[:, here] * env + latent[:, here] * d_env
        return carry

    lax.fori_loop(0, K // STEP, slope_of_latents, 0, unroll=4)

    spread2 = jnp.concatenate([spread, spread], axis=1)
    for part, (first, last) in enumerate(MOMENT_PARTS):
        cols = slice(first * C, last * C)
        wait_part(mrecv, r2, part)
        hi, lo = split(mrecv[part][...])
        mom[:, cols] = mom[:, cols] + dot(spread2, jnp.concatenate([hi, lo], axis=0))

    levels = ((0, 1), (6, 9), (1, 6))
    sums = []
    for first, last in levels:
        total = None
        for at in range(first, last):
            value = mom[:, at * C : (at + 1) * C]
            total = value * value if total is None else total + value * value
        sums.append(total)
    packed = jnp.concatenate([jnp.log1p(x) for x in sums], axis=1).astype(bf16)
    inner_act = dot(packed, wo_ref[...])
    act, d_act = silu_parts(inner_act)
    row_live = jnp.where(sub < dom_ref[...], 1.0, 0.0)
    weighted = row_live * we_ref[...]
    own_energy = jnp.sum(jnp.sum(act * weighted, axis=0, keepdims=True), axis=1, keepdims=True)
    d_inv = dot_nt((d_act * weighted).astype(bf16), wo_ref[...]).astype(bf16).astype(f32)
    pick2 = jnp.concatenate([pick, pick], axis=1)
    scale = [2.0 * d_inv[:, i * C : (i + 1) * C] / (1.0 + sums[i]) for i in range(3)]
    which = (0, 2, 2, 2, 2, 2, 1, 1, 1)
    for part, (first, last) in enumerate(SLOPE_PARTS):
        for at in range(first, last):
            cols = slice(at * C, (at + 1) * C)
            value = mom[:, cols] * scale[which[at]]
            hi, lo = split(value)
            there = slice((at - first) * C, (at - first + 1) * C)
            slope_send[part][:, there] = dot(pick2, jnp.concatenate([hi, lo], axis=0))
            gt[cols, 0:A] = value.T.astype(bf16)
        if part < 2:
            for g in (1, 3, 2, 0):
                slope_copy(g, part).start()

    def stage_copy(stage, peer, slot):
        count, mine, where, buf, send, recv = stages[stage]
        return pltpu.make_async_remote_copy(
            src_ref=buf.at[mine],
            dst_ref=buf.at[slot],
            send_sem=send.at[0],
            recv_sem=recv.at[0],
            device_id=where(peer),
            device_id_type=MESH,
        )

    def stage_start(stage, value):
        count, mine, where, buf, send, recv = stages[stage]
        buf[mine] = value
        for s in range(1, count):
            stage_copy(stage, lax.rem(mine + s, count), mine).start()

    def stage_end(stage):
        count, mine, where, buf, send, recv = stages[stage]
        if count > 1:
            wait_bytes(buf.at[pl.ds(0, count - 1)], recv.at[0])
        total = buf[0]
        for i in range(1, count):
            total = total + buf[i]
        return total

    half = lax.broadcasted_iota(jnp.int32, (8, C), 0)
    pair = jnp.where(half == 0, own_energy, dom_ref[...].astype(f32))
    stage_start(0, pair)

    def pull(part, q, carry):
        first, last = SLOPE_PARTS[part]
        side = even if first < 6 else odd
        lanes = pl.ds(pl.multiple_of(q * PULL_WIDE, PULL_WIDE), PULL_WIDE)
        found = dot(gt[first * C : last * C, :], side[0:R, lanes])
        for s in range(PULL_STEP):
            k = q * PULL_STEP + s
            cols = pl.ds(pl.multiple_of(k * A, A), A)
            w, d_w = pres[:, cols], acts[:, cols]
            for at in range(first, last):
                base = (at - first) * C
                h = found[base : base + C, s * A : (s + 1) * A]
                spot = pl.ds(k * 16 + at, 1)
                if at:
                    ays[spot, :] = jnp.sum(h * w, axis=0, keepdims=True)
                bys[spot, :] = jnp.sum(h * d_w, axis=0, keepdims=True)
        return carry

    def pull_all(part):
        step = functools.partial(pull, part)
        lax.fori_loop(0, K // PULL_STEP, step, 0, unroll=8)

    for part, (first, last) in enumerate(SLOPE_PARTS):
        wait_part(slope_recv, r3, part)
        for later in ((2,), (3,), (), ())[part]:
            for g in (1, 3, 2, 0):
                slope_copy(g, later).start()
        for at in range(first, last):
            cols = slice(at * C, (at + 1) * C)
            there = slice((at - first) * C, (at - first + 1) * C)
            gt[cols, A : 2 * A] = slope_recv[part][0:A, there].T.astype(bf16)
            gt[cols, 2 * A : R] = slope_recv[part][A:NG, there].T.astype(bf16)
        pull_all(part)
        if part == 1:
            stage_start(1, stage_end(0))
    stage_start(2, stage_end(1))

    g_of = {m: ays[pl.ds(at, K, stride=16), :] for at, m in enumerate(ORDER) if m}
    d_radius = bys[pl.ds(0, K, stride=16), :]
    for at in range(1, 9):
        d_radius = d_radius + bys[pl.ds(at, K, stride=16), :] * harm[at]
    inv, ux, uy, uz = geom[2], geom[3], geom[4], geom[5]
    dux = root3 * g_of[1] + root15 * (uy * g_of[4] + uz * g_of[7] + ux * g_of[8])
    duy = root3 * g_of[2] + root15 * (ux * g_of[4] + uz * g_of[5] - uy * g_of[8])
    duz = root3 * g_of[3] + root15 * (uy * g_of[5] + ux * g_of[7]) + 3.0 * root5 * uz * g_of[6]
    along = d_radius - (dux * ux + duy * uy + duz * uz) * inv
    for c, (du, u) in enumerate(((dux, ux), (duy, uy), (duz, uz))):
        value = du * inv + u * along
        hi = value.astype(bf16).astype(f32)
        brow[pl.ds(c, K, stride=NB), :] = hi
        brow[pl.ds(c + 3, K, stride=NB), :] = value - hi
    brow[pl.ds(6, K, stride=NB), :] = jnp.zeros((K, A), f32)
    brow[pl.ds(7, K, stride=NB), :] = jnp.zeros((K, A), f32)
    for k in range(K):
        ddr[:, k * A : (k + 1) * A] = brow[k * NB : (k + 1) * NB, :].astype(bf16)
    found = dot_nt(odd[0:R, :], ddr[...])
    wide_found = jnp.concatenate([found, jnp.zeros((R, A - 8), f32)], axis=1)
    full = jnp.concatenate([wide_found, jnp.zeros((3 * A - R, A), f32)], axis=0)
    flipped = [full[i * A : (i + 1) * A].T[0:8] for i in range(3)]
    fsend[0] = flipped[1]
    fsend[1] = flipped[2]

    def force_copy(g):
        return pltpu.make_async_remote_copy(
            src_ref=fsend.at[g // 2],
            dst_ref=frecv.at[g],
            send_sem=s4.at[0],
            recv_sem=r4.at[0],
            device_id=owners[g],
            device_id_type=MESH,
        )

    for g in (1, 3, 2, 0):
        force_copy(g).start()
    wait_bytes(frecv, r4.at[0])
    wide8 = lax.broadcasted_iota(jnp.int32, (8, A), 1)
    back_a = jnp.where(wide8 < GF, frecv[0], frecv[1])
    back_b = jnp.where(wide8 < GC, frecv[2], frecv[3])
    back = jnp.concatenate([back_a, back_b[:, 0 : 2 * GC]], axis=1)
    back = back + 0.0
    hi, lo = split(back)
    total = flipped[0] + dot(hi, pick) + dot(lo, pick)
    for c in range(3):
        force_out[c] = -(total[c : c + 1] + total[c + 3 : c + 4])
    sums = stage_end(2)
    energy_out[...] = sums[0:1, 0:1] / sums[1:2, 0:1]
    outs = [
        pltpu.make_async_copy(force_out, force_ref, out_sem.at[0]),
        pltpu.make_async_copy(energy_out, energy_ref, out_sem.at[1]),
    ]
    for out in outs:
        out.start()

    for out in outs:
        out.wait()
    wait_bytes(outf, s1.at[0])
    wait_bytes(outc, s1.at[1])
    wait_bytes(frecv, s4.at[0])
    for part in range(len(MOMENT_PARTS)):
        wait_part(msend, s2, part)
    for part in range(len(SLOPE_PARTS)):
        wait_part(slope_send, s3, part)
    for count, mine, where, buf, send, recv in stages:
        if count > 1:
            wait_bytes(buf.at[pl.ds(0, count - 1)], send.at[0])


def on_device(
    sizes,
    features,
    positions,
    neighbours,
    neighbour_counts,
    domain_counts,
    face_lists,
    corner_lists,
    w_center,
    w_neigh,
    w_radial,
    w_latent,
    w_readout,
    w_energy,
):
    nx, ny = sizes
    inner = min(nx, 8)
    outer = nx // inner
    vmem = pltpu.VMEM
    dma = pltpu.SemaphoreType.DMA

    def held(parts):
        return tuple(vmem((NG, (last - first) * C), f32) for first, last in parts)

    scratch = [
        vmem((A, C), bf16),
        vmem((3, 1, A), f32),
        vmem((K, A), jnp.int32),
        vmem((1, A), jnp.int32),
        vmem((1, 1), jnp.int32),
        vmem((2, GF), jnp.int32),
        vmem((2, GC), jnp.int32),
        vmem((C, C), bf16),
        vmem((C, C), bf16),
        vmem((NB, C), f32),
        vmem((C, C), bf16),
        vmem((3 * C, C), bf16),
        vmem((1, C), f32),
        dma((13,)),
        vmem((3, 1, A), f32),
        vmem((1, 1), f32),
        dma((2,)),
        vmem((2, GF + 8, C), f32),
        vmem((2, GC + 8, C), f32),
        vmem((2, GF + 8, C), f32),
        vmem((2, GC + 8, C), f32),
        vmem((3 * A, C), f32),
        vmem((C, 3 * A), bf16),
        vmem((C, A), f32),
        vmem((R + 4 * NB, PAIRS), bf16),
        vmem((R, PAIRS), bf16),
        vmem((K * NB, A), f32),
        vmem((K * NB, A), f32),
        vmem((4 * NB, PAIRS), bf16),
        vmem((9, K, A), f32),
        vmem((9, K, 16, A), bf16),
        vmem((6, K, A), f32),
        vmem((C, PAIRS), f32),
        vmem((C, PAIRS), f32),
        vmem((9 * C, PAIRS), bf16),
        vmem((A, 9 * C), f32),
        held(MOMENT_PARTS),
        held(MOMENT_PARTS),
        held(SLOPE_PARTS),
        held(SLOPE_PARTS),
        vmem((9 * C, R), bf16),
        vmem((K * 16, A), f32),
        vmem((K * 16, A), f32),
        vmem((8, PAIRS), bf16),
        vmem((2, 8, A), f32),
        vmem((4, 8, A), f32),
        vmem((inner, 8, C), f32),
        vmem((outer, 8, C), f32),
        vmem((ny, 8, C), f32),
        dma((2,)),
        dma((2,)),
        dma((len(MOMENT_PARTS),)),
        dma((len(MOMENT_PARTS),)),
        dma((len(SLOPE_PARTS),)),
        dma((len(SLOPE_PARTS),)),
        dma((1,)),
        dma((1,)),
        dma((1,)),
        dma((1,)),
        dma((1,)),
        dma((1,)),
        dma((1,)),
        dma((1,)),
    ]
    energy, forces = pl.pallas_call(
        functools.partial(kernel, sizes),
        out_shape=(
            jax.ShapeDtypeStruct((1, 1), f32),
            jax.ShapeDtypeStruct((3, 1, A), f32),
        ),
        in_specs=[pl.BlockSpec(memory_space=pltpu.HBM)] * 13,
        out_specs=(
            pl.BlockSpec(memory_space=pl.ANY),
            pl.BlockSpec(memory_space=pl.ANY),
        ),
        scratch_shapes=scratch,
        compiler_params=pltpu.CompilerParams(
            collective_id=0, has_side_effects=True, vmem_limit_bytes=61900 * 1024
        ),
    )(
        features[0, 0],
        jnp.transpose(positions, (0, 2, 1, 3))[0],
        neighbours[0, 0],
        neighbour_counts[0],
        domain_counts,
        face_lists[0, 0],
        corner_lists[0, 0],
        w_center,
        w_neigh,
        w_radial,
        w_latent,
        w_readout,
        w_energy[None, :],
    )
    return (energy.reshape(()), -jnp.transpose(forces[None], (0, 2, 1, 3)))


def solution(mesh):
    sizes = (mesh.shape["gx"], mesh.shape["gy"])
    placed = (
        P("gx", "gy", None, None),
        P("gx", "gy", None, None),
        P("gx", "gy", None, None),
        P("gx", "gy", None),
        P("gx", "gy"),
        P("gx", "gy", None, None),
        P("gx", "gy", None, None),
        P(),
        P(),
        P(),
        P(),
        P(),
        P(),
    )
    return jax.shard_map(
        functools.partial(on_device, sizes),
        mesh=mesh,
        in_specs=placed,
        out_specs=(P(), P("gx", "gy", None, None)),
        check_vma=False,
    )
```
